512 devices in a mesh: gx: 16 (over x, y), gy: 4 (over z_hi), gz: 8 (over z_lo, core).
Axes of the slice: x: 4, y: 4, z: 16 (z_hi: 4, z_lo: 4; z = z_hi * 4 + z_lo), core: 2. Of those that a mesh axis runs over, the one named last changes fastest.
Arguments:
- scalars: float32 [20, 524288], P(None, ('gx', 'gy', 'gz')), may hold values from -6 to 6
- particle_mass: float32 [524288], P(('gx', 'gy', 'gz')), may hold values from 0.5 to 2
- cell_first: int32 [524288], P(('gx', 'gy', 'gz')), may hold values from 0 to 511
- cell_second: int32 [524288], P(('gx', 'gy', 'gz')), may hold values from 0 to 511
- cell_final: int32 [524288], P(('gx', 'gy', 'gz')), may hold values from 0 to 511
- offset_first: float32 [3, 524288], P(None, ('gx', 'gy', 'gz')), may hold values from -0.5 to 0.5
- offset_second: float32 [3, 524288], P(None, ('gx', 'gy', 'gz')), may hold values from -0.5 to 0.5
- face_first: int32 [524288], P(('gx', 'gy', 'gz')), may hold values from 0 to 6, as said below
- face_second: int32 [524288], P(('gx', 'gy', 'gz')), may hold values from 0 to 6, as said below
- mean_field: float32 [20, 128, 32, 64], P(None, 'gx', 'gy', 'gz'), may hold values from -6 to 6
- mix_rate: float32 [128, 32, 64], P('gx', 'gy', 'gz'), may hold values from 0.25 to 2
- react_in: float32 [128, 20], replicated, may hold values from -1.25 to 1.25
- hidden_bias: float32 [128], replicated, may hold values from -4 to 4
- react_out: float32 [20, 128], replicated, may hold values from -0.5 to 0.5
Outputs:
- cell_mean: float32 [20, 128, 32, 64], P(None, 'gx', 'gy', 'gz')
The draws below stay inside these ranges and needn't reach their ends.
Inputs may be any that keep to these rules, and one draw needn't show every extreme that they name: `face_first`: on one owner at most 64 particles carry the same nonzero code, and some owner has exactly 64 with one code. A particle with a nonzero face_first has face_second 0; on one owner at most 64 particles carry the same nonzero code, and some owner has exactly 64 with one code.
All inputs are finite; a program needn't handle non-finite values.
Results may differ from the reference program's by a relative error of at most 0.00005.
Values sent between devices are 32-bit elements; how exact they have to be, the bound alone decides.
A program may use at most 64 MiB of HBM per device.

```python
import math
import jax
import jax.numpy as jnp
from jax import lax

S = 20
H = 128
CX = 8
CY = 8
CZ = 8
P_DEV = 1024
BLOCK = 64
CELLS = 512
P_TOTAL = 524288
NX = 128
NY = 32
NZ = 64
N_GX = 16
N_GY = 4
N_GZ = 8


def face_pair(key):
    owners_all = P_TOTAL // P_DEV
    capacity = BLOCK
    key_level, key_full, key_counts, key_face, key_shuffle = jax.random.split(key, 5)
    load_level = jax.random.randint(key_level, (2, owners_all), capacity // 4, capacity + 1)
    full_device = jax.random.randint(key_full, (2,), 0, owners_all)
    load_level = jnp.where(jnp.arange(owners_all)[None, :] == full_device[:, None], capacity, load_level)
    face_counts = jax.random.randint(key_counts, (2, owners_all, 6), 0, capacity + 1)
    face_counts = face_counts * load_level[..., None] // capacity
    full_face = jax.random.randint(key_face, (2, owners_all), 0, 6)
    face_counts = jnp.where(jnp.arange(6)[None, None, :] == full_face[..., None], load_level[..., None], face_counts)
    position = jnp.arange(P_DEV)
    bound_first = jnp.cumsum(face_counts[0], axis=1)
    total_first = bound_first[:, -1:]
    code_first = 1 + jnp.sum((position[None, :, None] >= bound_first[:, None, :]).astype(jnp.int32), axis=2)
    code_first = jnp.where(position[None, :] < total_first, code_first, 0)
    bound_second = total_first + jnp.cumsum(face_counts[1], axis=1)
    code_second = 1 + jnp.sum((position[None, :, None] >= bound_second[:, None, :]).astype(jnp.int32), axis=2)
    in_second = (position[None, :] >= total_first) & (position[None, :] < bound_second[:, -1:])
    code_second = jnp.where(in_second, code_second, 0)
    shuffles = jax.vmap(lambda single: jax.random.permutation(single, P_DEV))(jax.random.split(key_shuffle, owners_all))
    code_first = jnp.take_along_axis(code_first, shuffles, axis=1)
    code_second = jnp.take_along_axis(code_second, shuffles, axis=1)
    return (code_first.reshape(-1).astype(jnp.int32), code_second.reshape(-1).astype(jnp.int32))


def draw_face_first(key, part):
    return face_pair(key)[0]


def draw_face_second(key, part):
    return face_pair(key)[1]


def place_ends(result, rng, smallest, high):
    dims = result.shape
    spot = [jax.random.randint(jax.random.fold_in(rng, axis), (), 0, dims[axis]) for axis in range(len(dims))]
    result = result.at[tuple(spot)].set(smallest)
    longest = dims.index(max(dims))
    spot[longest] = (spot[longest] + 1) % dims[longest]
    return result.at[tuple(spot)].set(high)


def block_scale(key, dims, cuts, smallest, largest):
    def one(axis_at, shards_of):
        draws = jax.random.uniform(jax.random.fold_in(jax.random.fold_in(key, 6), axis_at), (shards_of,), jnp.float32, smallest / len(cuts), largest / len(cuts))
        return jnp.repeat(jnp.exp(draws), dims[axis_at] // shards_of).reshape((-1,) + (1,) * (len(dims) - axis_at - 1))

    factor_of = one(*cuts[0])
    for cut in cuts[1:]:
        factor_of = factor_of * one(*cut)
    return factor_of


def scatter_about(own_key, shape, scale, limit, cuts=(), held_as=jnp.bfloat16):
    array = scale * jax.random.normal(own_key, shape, jnp.float32)
    if cuts:
        array = array * block_scale(own_key, shape, cuts, -0.22, 0.18)
    return jnp.clip(array, -limit, limit).astype(held_as)


def setup_inputs(seed: int = 0) -> dict:
    streams_of = jax.random.split(jax.random.key(seed), 15)
    return {
        "scalars": scatter_about(streams_of[0], (S, P_TOTAL), 1.0, 6.0, ((1, 512),), jnp.float32),
        "particle_mass": jnp.clip(jnp.exp(math.log(2.0) - 1.3862944 * jax.random.uniform(streams_of[1], (P_TOTAL,), jnp.float32) ** block_scale(streams_of[1], (P_TOTAL,), ((0, 512),), -0.2, 0.2)), 0.5, 2.0),
        "cell_first": place_ends(jax.random.randint(streams_of[2], (P_TOTAL,), 0, CELLS), jax.random.fold_in(streams_of[2], 1), 0, CELLS - 1).astype(jnp.int32),
        "cell_second": place_ends(jax.random.randint(streams_of[3], (P_TOTAL,), 0, CELLS), jax.random.fold_in(streams_of[3], 1), 0, CELLS - 1).astype(jnp.int32),
        "cell_final": place_ends(jax.random.randint(streams_of[4], (P_TOTAL,), 0, CELLS), jax.random.fold_in(streams_of[4], 1), 0, CELLS - 1).astype(jnp.int32),
        "offset_first": jnp.clip(jax.random.uniform(streams_of[5], (3, P_TOTAL), jnp.float32, -0.5, 0.5) * block_scale(streams_of[5], (3, P_TOTAL), ((1, 512),), -0.4, 0.0), -0.5, 0.5),
        "offset_second": jnp.clip(jax.random.uniform(streams_of[6], (3, P_TOTAL), jnp.float32, -0.5, 0.5) * block_scale(streams_of[6], (3, P_TOTAL), ((1, 512),), -0.4, 0.0), -0.5, 0.5),
        "face_first": draw_face_first(jax.random.fold_in(streams_of[14], 71), 0),
        "face_second": draw_face_second(jax.random.fold_in(streams_of[14], 71), 0),
        "mean_field": scatter_about(streams_of[9], (S, NX, NY, NZ), 1.0, 6.0, ((1, 16), (2, 4), (3, 8)), jnp.float32),
        "mix_rate": jnp.clip(jnp.exp(math.log(2.0) - 2.0794415 * jax.random.uniform(streams_of[10], (NX, NY, NZ), jnp.float32) ** block_scale(streams_of[10], (NX, NY, NZ), ((0, 16), (1, 4), (2, 8)), -0.2, 0.2)), 0.25, 2.0),
        "react_in": scatter_about(streams_of[11], (H, S), S ** -0.5, 1.25, (), jnp.float32),
        "hidden_bias": scatter_about(streams_of[12], (H,), 1.0, 4.0, (), jnp.float32),
        "react_out": scatter_about(streams_of[13], (S, H), H ** -0.5, 0.5, (), jnp.float32),
    }


IEM_FACTOR = 0.4
TIME_STEP = 0.4
PRIOR_MASS = 2.0


def spline(position):
    return (0.5 * (0.5 - position) ** 2, 0.75 - position * position, 0.5 * (0.5 + position) ** 2)


def interpolate(flat_field, base_index, strides, offsets):
    along_x = spline(offsets[0])
    along_y = spline(offsets[1])
    along_z = spline(offsets[2])
    terms = []
    for step_a in range(3):
        for step_b in range(3):
            for step_e in range(3):
                flat_shift = (step_a - 1) * strides[0] + (step_b - 1) * strides[1] + (step_e - 1)
                weight = along_x[step_a] * along_y[step_b] * along_z[step_e]
                terms.append(weight[None, :] * jnp.take(flat_field, base_index + flat_shift, axis=1))
    return sum(terms[1:], terms[0])


def mixing(values, sampled):
    count_s = values.shape[0]
    return values - IEM_FACTOR * sampled[count_s][None, :] * (values - sampled[:count_s])


def reaction(values, react_in, hidden_bias, react_out):
    hidden = jnp.tanh(jnp.dot(react_in, values, precision=lax.Precision.HIGHEST) + hidden_bias[:, None])
    return values + TIME_STEP * jnp.dot(react_out, hidden, precision=lax.Precision.HIGHEST)


def cell_average(values, masses, cells, field_now):
    ncells = field_now.shape[1] * field_now.shape[2] * field_now.shape[3]
    weighted = jax.ops.segment_sum((values * masses[None, :]).T, cells, num_segments=ncells)
    weights_sum = jax.ops.segment_sum(masses, cells, num_segments=ncells)
    return (weighted.T.reshape(field_now.shape) + PRIOR_MASS * field_now) / (weights_sum.reshape(field_now.shape[1:])[None] + PRIOR_MASS)


def pad_field(field_now):
    wrapped = jnp.concatenate([field_now[..., -1:], field_now, field_now[..., :1]], axis=3)
    padded = jnp.pad(wrapped, ((0, 0), (1, 1), (1, 1), (0, 0)))
    return padded.reshape(padded.shape[0], -1)


def global_coords(owner_x, owner_y, owner_z, cells):
    cell_x = cells // (CY * CZ)
    cell_y = (cells // CZ) % CY
    cell_z = cells % CZ
    return owner_x * CX + cell_x, owner_y * CY + cell_y, owner_z * CZ + cell_z


def moved(owner_x, owner_y, owner_z, faces):
    new_x = owner_x + (faces == 1).astype(jnp.int32) - (faces == 2).astype(jnp.int32)
    new_y = owner_y + (faces == 3).astype(jnp.int32) - (faces == 4).astype(jnp.int32)
    new_z = (owner_z + (faces == 5).astype(jnp.int32) - (faces == 6).astype(jnp.int32) + N_GZ) % N_GZ
    inside = (new_x >= 0) & (new_x < N_GX) & (new_y >= 0) & (new_y < N_GY)
    return jnp.clip(new_x, 0, N_GX - 1), jnp.clip(new_y, 0, N_GY - 1), new_z, inside


def sample_at(flat_field, owners, cells, offsets):
    strides = ((NY + 2) * (NZ + 2), NZ + 2)
    glob_x, glob_y, glob_z = global_coords(owners[0], owners[1], owners[2], cells)
    base_index = (glob_x + 1) * strides[0] + (glob_y + 1) * strides[1] + glob_z + 1
    return interpolate(flat_field, base_index.astype(jnp.int32), strides, offsets)


def segment_ids(owners, cells):
    glob_x, glob_y, glob_z = global_coords(owners[0], owners[1], owners[2], cells)
    return ((glob_x * NY + glob_y) * NZ + glob_z).astype(jnp.int32)


def reference(scalars, particle_mass, cell_first, cell_second, cell_final, offset_first, offset_second, face_first, face_second, mean_field, mix_rate, react_in, hidden_bias, react_out):
    device = jnp.arange(P_TOTAL, dtype=jnp.int32) // P_DEV
    owners = (device // (N_GY * N_GZ), (device // N_GZ) % N_GY, device % N_GZ)
    flat_first = pad_field(jnp.concatenate([mean_field, mix_rate[None]], axis=0))
    sampled_first = sample_at(flat_first, owners, cell_first, offset_first)
    reacted_first = reaction(mixing(scalars, sampled_first), react_in, hidden_bias, react_out)
    next_x, next_y, next_z, inside_first = moved(owners[0], owners[1], owners[2], face_first)
    mass_first = particle_mass * inside_first.astype(jnp.float32)
    owners_second = (next_x, next_y, next_z)
    field_second = cell_average(reacted_first, mass_first, segment_ids(owners_second, cell_second), mean_field)
    flat_second = pad_field(jnp.concatenate([field_second, mix_rate[None]], axis=0))
    sampled_second = sample_at(flat_second, owners_second, cell_second, offset_second)
    reacted_second = reaction(mixing(reacted_first, sampled_second), react_in, hidden_bias, react_out)
    last_x, last_y, last_z, inside_second = moved(next_x, next_y, next_z, face_second)
    mass_second = mass_first * inside_second.astype(jnp.float32)
    return cell_average(reacted_second, mass_second, segment_ids((last_x, last_y, last_z), cell_final), field_second)
```

```python
import functools

import jax
import jax.numpy as jnp
from jax import lax
from jax.experimental import pallas as pl
from jax.experimental.pallas import tpu as pltpu
from jax.sharding import PartitionSpec as P

MESH = pl.DeviceIdType.MESH
F32 = jnp.float32
BF16 = jnp.bfloat16

IEM_FACTOR = 0.4
TIME_STEP = 0.4
PRIOR_MASS = 2.0

ROWS = 24
LANES = 32
SIDE = 8
PLANE = 64
BLOCK = 64

NAMES = [
    "scalars",
    "particle_mass",
    "cell_first",
    "cell_second",
    "cell_final",
    "offset_first",
    "offset_second",
    "face_first",
    "face_second",
    "mean_field",
    "mix_rate",
    "react_in",
    "hidden_bias",
    "react_out",
]
INPUTS = len(NAMES)
ORDER = ["mean_field", "mix_rate", "cell_first", "offset_first", "react_in", "hidden_bias"]
ORDER += ["react_out", "face_first", "face_second", "cell_second", "cell_final"]
ORDER += ["particle_mass", "offset_second", "scalars"]

MOVE_STEPS = [(1, 0, 0), (-1, 0, 0), (0, 1, 0), (0, -1, 0), (0, 0, 1), (0, 0, -1)]

OWN = [slice(i, i + 256) for i in range(0, 1024, 256)]
NEW = [slice(0, 256), slice(256, 384)]

NT = (((1,), (1,)), ((), ()))


def dot(a, b):
    return jnp.dot(a, b, preferred_element_type=F32)


def dot_nt(a, b):
    return lax.dot_general(a, b, NT, preferred_element_type=F32)


def parts(v):
    high = v.astype(BF16)
    return high, (v - high.astype(F32)).astype(BF16)


def parts_wide(v):
    high = v.astype(BF16).astype(F32)
    return high, v - high


def iota(shape, dim):
    return lax.broadcasted_iota(jnp.int32, shape, dim)


def spline(u):
    return 0.5 * (0.5 - u) ** 2, 0.75 - u * u, 0.5 * (0.5 + u) ** 2


def along(cell, offset, low_ok, high_ok):
    low, mid, high = spline(offset)
    away = iota((SIDE, cell.shape[1]), 0) - cell
    inner = jnp.where(
        away == 0, mid, jnp.where(away == 1, high, jnp.where(away == -1, low, 0.0))
    )
    return (
        inner,
        jnp.where(cell == 0, low, 0.0) * low_ok,
        jnp.where(cell == SIDE - 1, high, 0.0) * high_ok,
    )


def weights(cells, offsets, ok):
    x_in, x_low, x_high = along(cells >> 6, offsets[0], ok[0], ok[1])
    y_in, y_low, y_high = along((cells >> 3) & 7, offsets[1], ok[2], ok[3])
    z_in, z_low, z_high = along(cells & 7, offsets[2], 1.0, 1.0)
    inner = jnp.concatenate([z_in * y_in[y : y + 1] for y in range(SIDE)], axis=0)
    row = iota(z_in.shape, 0)
    corner = jnp.where(
        row == 0,
        y_low * z_low,
        jnp.where(
            row == 1,
            y_low * z_high,
            jnp.where(row == 2, y_high * z_low, jnp.where(row == 3, y_high * z_high, 0.0)),
        ),
    )
    outer = jnp.concatenate(
        [z_in * y_low, z_in * y_high, y_in * z_low, y_in * z_high, corner, jnp.zeros_like(corner)],
        axis=0,
    )
    none = jnp.zeros((PLANE - outer.shape[0], cells.shape[1]), BF16)
    high, low = parts(outer)
    outer = jnp.concatenate([high, none, high, none, low, none], axis=0)
    return three_parts(*parts(inner)), outer, x_in, x_low, x_high


def compact(field):
    return jnp.concatenate([field[LANES * x : LANES * x + ROWS] for x in range(SIDE)], axis=0)


def spread(field):
    none = jnp.zeros((LANES - ROWS, field.shape[1]), field.dtype)
    pieces = []
    for x in range(SIDE):
        pieces += [field[ROWS * x : ROWS * (x + 1)], none]
    return jnp.concatenate(pieces, axis=0)


def three_parts(high, low):
    return jnp.concatenate([high, high, low], axis=0)


def left_of(field):
    high, low = parts_wide(field)
    return jnp.concatenate([high, low, high], axis=1).astype(BF16)


def left_outer(outer):
    high, low = parts_wide(outer)
    turned = jnp.concatenate([high, low], axis=0).T
    base = SIDE * LANES
    rows = jnp.concatenate(
        [
            compact(turned[:base]),
            turned[base + 3 * LANES : base + 3 * LANES + ROWS],
            turned[base : base + ROWS],
        ],
        axis=0,
    )
    return jnp.concatenate([rows, rows[:, :PLANE]], axis=1).astype(BF16)


def gather_own(result, x_in):
    total = x_in[0:1] * result[:ROWS]
    for x in range(1, SIDE):
        total = total + x_in[x : x + 1] * result[ROWS * x : ROWS * (x + 1)]
    return total


def gather_inner(left, w):
    return gather_own(dot(left, w[0]), w[2])


def gather_outer(lefts, w):
    result = dot(lefts[0], w[1])
    own = SIDE * ROWS
    sides = dot(lefts[1], w[0]) + result[own:]
    return gather_own(result[:own], w[2]) + w[3] * sides[:ROWS] + w[4] * sides[ROWS:]


def react(values, sampled, first, second):
    mixed = values - IEM_FACTOR * sampled[20:21] * (values - sampled)
    mixed = jnp.where(iota(mixed.shape, 0) == 20, 1.0, mixed)
    high, low = parts_wide(mixed)
    none = jnp.zeros((128 - 3 * ROWS, mixed.shape[1]), F32)
    stacked = jnp.concatenate([high, low, high, none], axis=0).astype(BF16)
    hidden_high, hidden_low = parts(jnp.tanh(dot(first, stacked)))
    result = dot(second, jnp.concatenate([hidden_high, hidden_low], axis=0))
    return mixed + TIME_STEP * (result[:ROWS] + result[ROWS:])


def slots_of(faces):
    count = faces.shape[1]
    code = iota((SIDE, count), 0)
    chosen = code + 1 == faces
    mask = jnp.where(chosen, 1.0, 0.0)
    chunks = count // 128
    stacked = jnp.concatenate(
        [mask[:, 128 * j : 128 * (j + 1)] for j in range(chunks)], axis=0
    ).astype(BF16)
    row, col = iota((128, 256), 0), iota((128, 256), 1)
    counter = jnp.where((row < col) | (col >= 128), 1.0, 0.0).astype(BF16)
    ranks = dot(stacked, counter)
    before = jnp.zeros((SIDE, 128), F32)
    pieces = []
    for j in range(chunks):
        rows = slice(SIDE * j, SIDE * (j + 1))
        pieces.append(ranks[rows, :128] + before)
        before = before + ranks[rows, 128:]
    rank = jnp.concatenate(pieces, axis=1)
    place = jnp.where(chosen, rank.astype(jnp.int32) + BLOCK * code + 1, 0)
    return jnp.sum(place, axis=0, keepdims=True) - 1


def one_hot(index, size):
    shape = (16, index.shape[1])
    away = iota(shape, 0).astype(F32).astype(BF16)
    away = away - jnp.broadcast_to(index.astype(F32), shape).astype(BF16)
    one, zero = jnp.ones(shape, BF16), jnp.zeros(shape, BF16)
    return jnp.concatenate(
        [jnp.where(away == jnp.full(shape, -16.0 * b, BF16), one, zero) for b in range(size // 16)],
        axis=0,
    )


def pack(payload, slots):
    high, low = parts_wide(payload)
    chosen = jnp.concatenate([one_hot(slots, 256), one_hot(slots - 256, 128)], axis=0)
    return dot_nt(jnp.concatenate([high, low], axis=0).astype(BF16), chosen)


def scatter(values, masses, cells):
    high, low = parts_wide(values * masses)
    stacked = jnp.concatenate([high, low], axis=0)
    upper = (cells >> 8).astype(F32)
    left = jnp.concatenate([stacked * (1.0 - upper), stacked * upper], axis=0)
    return dot_nt(left.astype(BF16), one_hot(cells & 255, 4 * PLANE))


def by_cell(result):
    pieces = []
    for x in range(SIDE):
        base = 2 * ROWS * (x // 4)
        lanes = slice(PLANE * (x % 4), PLANE * (x % 4 + 1))
        pieces.append(result[base : base + ROWS, lanes] + result[base + ROWS : base + 2 * ROWS, lanes])
    return jnp.concatenate(pieces, axis=0)


def average(sums, field):
    pieces = []
    for x in range(SIDE):
        rows = slice(ROWS * x, ROWS * (x + 1))
        one, old = sums[rows], field[rows]
        new = (one + PRIOR_MASS * old) / (one[20:21] + PRIOR_MASS)
        pieces.append(jnp.where(iota(new.shape, 0) == 20, old, new))
    return jnp.concatenate(pieces, axis=0)


def kernel(sizes, *refs):
    inputs, out_ref, refs = refs[:INPUTS], refs[INPUTS], refs[INPUTS + 1 :]
    local, refs = refs[:INPUTS], refs[INPUTS:]
    (
        plane,
        z_send,
        c_send,
        x_send,
        face_got,
        corner_got,
        edge_got,
        point_got,
        x_got,
        packed,
        got,
        rows_buf,
        pay,
        local_sem,
        halo_send_sem,
        halo_recv_sem,
        move_send_sem,
        move_recv_sem,
    ) = refs
    n_gx, n_gy, n_gz = sizes
    gx, gy, gz = lax.axis_index("gx"), lax.axis_index("gy"), lax.axis_index("gz")

    def three(index, size):
        return {-1: lax.rem(index + size - 1, size), 0: index, 1: lax.rem(index + 1, size)}

    near_x, near_y, near_z = three(gx, n_gx), three(gy, n_gy), three(gz, n_gz)

    def at(dx, dy, dz):
        return near_x[dx], near_y[dy], near_z[dz]

    faces = [(1, 0), (-1, 0), (0, 1), (0, -1)]
    corners = [(1, 1), (1, -1), (-1, 1), (-1, -1)]
    x_steps = [1, -1]
    halo_steps = [(0, dy, dz) for dy, dz in faces + corners]
    halo_steps += [(dx, dy, dz) for dx in x_steps for dy, dz in faces + corners]
    halo_steps += [(dx, 0, 0) for dx in x_steps]

    loads = {
        name: pltpu.make_async_copy(a, to, local_sem.at[i])
        for i, (name, a, to) in enumerate(zip(NAMES, inputs, local))
    }
    for name in ORDER[:2]:
        loads[name].start()
    barrier = pltpu.get_barrier_semaphore()
    for step in halo_steps:
        pl.semaphore_signal(barrier, inc=1, device_id=at(*step), device_id_type=MESH)
    for name in ORDER[2:]:
        loads[name].start()

    def load(name):
        loads[name].wait()
        return local[NAMES.index(name)]

    def remote(src, dst, send_sem, recv_sem, step):
        copy = pltpu.make_async_remote_copy(
            src_ref=src,
            dst_ref=dst,
            send_sem=send_sem,
            recv_sem=recv_sem,
            device_id=at(*step),
            device_id_type=MESH,
        )
        copy.start()
        return copy

    def put(h, value):
        plane[h, 0] = value[:, :128]
        plane[h, 1] = value[:, 128:]

    def send_halo(h, first, source, target):
        return [
            remote(
                src,
                dst,
                halo_send_sem.at[h, first + i],
                halo_recv_sem.at[h, first + i],
                halo_steps[first + i],
            )
            for i, (src, dst) in enumerate(zip(source, target))
        ]

    def send_x(h, field):
        x_send[h, 0, :, 0:PLANE] = field[7 * ROWS : 8 * ROWS]
        x_send[h, 1, :, 0:PLANE] = field[0:ROWS]
        return send_halo(h, 24, [x_send.at[h, k] for k in range(2)], [x_got.at[h, k] for k in range(2)])

    def send_plane(h):
        for z, slot in ((7, 0), (0, 1)):
            for half in range(2):
                z_send[h, slot, half] = plane[h, half, pl.ds(z, SIDE, stride=SIDE), :]
        for slot, row in enumerate((63, 56, 7, 0)):
            for half in range(2):
                c_send[h, slot, half] = plane[h, half, row : row + 1, :]
        rows = plane.at[h]
        source = [rows.at[:, 56:64], rows.at[:, 0:8], z_send.at[h, 0], z_send.at[h, 1]]
        source += [c_send.at[h, slot] for slot in range(4)]
        target = [face_got.at[h, slot] for slot in range(4)]
        target += [corner_got.at[h, slot] for slot in range(4)]
        for k, half in ((0, 1), (1, 0)):
            source += [rows.at[half, 56:64], rows.at[half, 0:8]]
            source += [z_send.at[h, slot, half] for slot in range(2)]
            source += [c_send.at[h, slot, half] for slot in range(4)]
            target += [edge_got.at[h, k, slot] for slot in range(4)]
            target += [point_got.at[h, k, slot] for slot in range(4)]
        return send_halo(h, 0, source, target)

    def stack_outer(face, corner):
        row = iota((SIDE, 128), 0)
        last = jnp.zeros((SIDE, 128), F32)
        for slot in range(4):
            last = jnp.where(row == slot, corner[slot], last)
        none = jnp.zeros((PLANE - 5 * SIDE, 128), F32)
        return jnp.concatenate(face + [last, none], axis=0)

    def halo(h, copies):
        for copy in copies:
            copy.wait_recv()
        both = [
            stack_outer(
                [face_got[h, slot, half] for slot in range(4)],
                [corner_got[h, slot, half] for slot in range(4)],
            )
            for half in range(2)
        ]
        side = [
            stack_outer(
                [edge_got[h, k, slot] for slot in range(4)],
                [point_got[h, k, slot] for slot in range(4)],
            )
            for k in range(2)
        ]
        last = jnp.where(iota((PLANE, 128), 1) < PLANE, side[1], side[0])
        planes = left_outer(jnp.concatenate(both + [last], axis=1))
        sides = jnp.concatenate([x_got[h, 0], x_got[h, 1]], axis=0)[:, :PLANE]
        return planes, left_of(sides)

    lower = iota((16, 128), 1) < BLOCK

    def turned(value):
        return pltpu.roll(value, BLOCK, 1)

    def send_moves(m, block):
        copies = []
        for t in (1, 0, 2):
            tile = block[:, 128 * t : 128 * (t + 1)]
            packed[m, 2 * t] = jnp.where(lower, tile[:16], turned(tile[16:]))
            packed[m, 2 * t + 1] = jnp.where(lower, turned(tile[:16]), tile[16:])
            for k in (2 * t, 2 * t + 1):
                copies.append(
                    remote(
                        packed.at[m, k],
                        got.at[m, k],
                        move_send_sem.at[m, k],
                        move_recv_sem.at[m, k],
                        MOVE_STEPS[k],
                    )
                )
        return copies

    def arrivals(m, copies):
        for copy in copies:
            copy.wait_recv()
        tiles = []
        for t in range(3):
            one, two = got[m, 2 * t], got[m, 2 * t + 1]
            top = jnp.where(lower, one, turned(two))
            bottom = jnp.where(lower, turned(one), two)
            tiles.append(jnp.concatenate([top, bottom], axis=0))
        return jnp.concatenate(tiles, axis=1)

    plane[0] = jnp.zeros((2, PLANE, 128), F32)
    x_send[...] = jnp.zeros(x_send.shape, F32)
    same_z = jnp.where(iota((PLANE, SIDE), 0) & 7 == iota((PLANE, SIDE), 1), 1.0, 0.0)
    same_y = iota((PLANE, PLANE), 0) >> 3 == iota((PLANE, PLANE), 1) & 7
    goes = (iota((PLANE, SIDE * LANES), 0) >> 3) * LANES + 20
    goes = jnp.where(iota((PLANE, SIDE * LANES), 1) == goes, 1.0, 0.0).astype(BF16)
    rate = jnp.zeros((PLANE, SIDE * LANES), F32)
    for part in parts(load("mix_rate")[...]):
        along_z = jnp.where(same_y, dot_nt(same_z.astype(BF16), part), 0.0)
        rate = rate + dot(along_z.astype(BF16), goes)
    mean_ref = load("mean_field")
    for x in range(SIDE):
        base = LANES * (x % 4)
        plane[0, x // 4, :, base : base + 20] = mean_ref[PLANE * x : PLANE * (x + 1), :]
    inner1 = jnp.concatenate([plane[0, 0], plane[0, 1]], axis=1) + rate
    put(0, inner1)

    pl.semaphore_wait(barrier, len(halo_steps))
    halo_copies1 = send_plane(0)
    field1 = compact(inner1.T)
    halo_copies1 = halo_copies1 + send_x(0, field1)

    ok = [
        jnp.where(gx > 0, 1.0, 0.0),
        jnp.where(gx < n_gx - 1, 1.0, 0.0),
        jnp.where(gy > 0, 1.0, 0.0),
        jnp.where(gy < n_gy - 1, 1.0, 0.0),
    ]

    cell1 = load("cell_first")
    off1 = load("offset_first")
    face1 = load("face_first")
    cell2 = load("cell_second")
    cell3 = load("cell_final")
    mass = load("particle_mass")
    off2 = load("offset_second")
    pay[0:20, :] = load("scalars")[...]
    pay[20:21, :] = mass[...]
    pay[21:24, :] = off2[...]
    pay[24:25, :] = cell2[...].astype(F32)
    pay[25:26, :] = cell3[...].astype(F32)
    pay[26:27, :] = cell1[...].astype(F32)
    pay[27:30, :] = off1[...]
    pay[30:32, :] = jnp.zeros((2, pay.shape[1]), F32)

    def packed_movers(faces):
        slots = slots_of(faces)
        block = sum(pack(pay[:, lanes], slots[:, lanes]) for lanes in OWN)
        return block[:32] + block[32:]

    def weights_at(cells, offsets, lanes):
        return weights(cells[:, lanes], [offsets[d : d + 1, lanes] for d in range(3)], ok)

    def scalars_of(block):
        row = iota((ROWS, block.shape[1]), 0)
        return jnp.where(row == 20, 1.0, jnp.where(row < 20, block[:ROWS], 0.0))

    def message(values, block):
        row = iota((ROWS, block.shape[1]), 0)
        return jnp.concatenate([jnp.where(row < 20, values, block[:ROWS]), block[ROWS:]], axis=0)

    def work(values, sampled, outer, w):
        return react(values, sampled + gather_outer(outer, w), first, second)

    movers = packed_movers(face1[...])
    mover_cells = movers[26:27].astype(jnp.int32)
    w_movers = [weights_at(mover_cells, movers[27:30], lanes) for lanes in NEW]

    left = left_of(field1)
    in_movers = [gather_inner(left, w) for w in w_movers]

    rows_buf[...] = jnp.zeros(rows_buf.shape, F32)
    rows_buf[0, 0:20, :] = load("react_in")[...]
    rows_buf[0, 20:21, :] = load("hidden_bias")[...]
    rows_buf[1, 0:20, :] = load("react_out")[...]
    high, low = parts_wide(rows_buf[0])
    first = jnp.concatenate(
        [high, high, low, jnp.zeros((128 - 3 * ROWS, 128), F32)], axis=0
    ).T.astype(BF16)
    high, low = parts_wide(rows_buf[1])
    second = jnp.concatenate(
        [
            jnp.concatenate([high, high], axis=1),
            jnp.concatenate([low, jnp.zeros_like(low)], axis=1),
        ],
        axis=0,
    ).astype(BF16)

    w_own, in_own = [], []
    for lanes in OWN:
        w_own.append(weights_at(cell1, off1, lanes))
        in_own.append(gather_inner(left, w_own[-1]))

    outer = halo(0, halo_copies1)
    moved = [
        message(work(scalars_of(movers[:, lanes]), one, outer, w), movers[:, lanes])
        for lanes, one, w in zip(NEW, in_movers, w_movers)
    ]
    move_copies1 = send_moves(0, jnp.concatenate(moved, axis=1))

    values, sums = [], 0.0
    for lanes, one, w in zip(OWN, in_own, w_own):
        values.append(work(scalars_of(pay[:, lanes]), one, outer, w))
        stay = jnp.where(face1[:, lanes] == 0, mass[:, lanes], 0.0)
        sums = sums + scatter(values[-1], stay, cell2[:, lanes])
        pay[0:20, lanes] = values[-1][:20]

    came = arrivals(0, move_copies1)
    lane = iota((1, 6 * BLOCK), 1)
    alive = jnp.where(
        lane < 64,
        ok[0],
        jnp.where(lane < 128, ok[1], jnp.where(lane < 192, ok[2], jnp.where(lane < 256, ok[3], 1.0))),
    )
    came_values = [scalars_of(came[:, lanes]) for lanes in NEW]
    came_mass = came[20:21] * alive
    came_cell2 = came[24:25].astype(jnp.int32)
    came_cell3 = came[25:26].astype(jnp.int32)
    for lanes, one in zip(NEW, came_values):
        sums = sums + scatter(one, came_mass[:, lanes], came_cell2[:, lanes])
    field2 = average(by_cell(sums), field1)
    put(1, spread(field2).T)
    halo_copies2 = send_plane(1) + send_x(1, field2)

    face2 = load("face_second")
    movers = packed_movers(face2[...])
    mover_cells = movers[24:25].astype(jnp.int32)
    w_movers = [weights_at(mover_cells, movers[21:24], lanes) for lanes in NEW]

    left = left_of(field2)
    in_movers = [gather_inner(left, w) for w in w_movers]
    w_own, in_own = [], []
    for lanes in OWN:
        w_own.append(weights_at(cell2, off2, lanes))
        in_own.append(gather_inner(left, w_own[-1]))
    w_came, in_came = [], []
    for lanes in NEW:
        w_came.append(weights_at(came_cell2, came[21:24], lanes))
        in_came.append(gather_inner(left, w_came[-1]))

    outer = halo(1, halo_copies2)
    moved = [
        message(work(scalars_of(movers[:, lanes]), one, outer, w), movers[:, lanes])
        for lanes, one, w in zip(NEW, in_movers, w_movers)
    ]
    move_copies2 = send_moves(1, jnp.concatenate(moved, axis=1))

    sums = 0.0
    for lanes, old, one, w in zip(OWN, values, in_own, w_own):
        new = work(old, one, outer, w)
        stay = jnp.where(face1[:, lanes] + face2[:, lanes] == 0, mass[:, lanes], 0.0)
        sums = sums + scatter(new, stay, cell3[:, lanes])
    for lanes, old, one, w in zip(NEW, came_values, in_came, w_came):
        new = work(old, one, outer, w)
        sums = sums + scatter(new, came_mass[:, lanes], came_cell3[:, lanes])

    last = arrivals(1, move_copies2)
    last_mass = last[20:21] * alive
    last_cell = last[25:26].astype(jnp.int32)
    for lanes in NEW:
        sums = sums + scatter(scalars_of(last[:, lanes]), last_mass[:, lanes], last_cell[:, lanes])
    sums = by_cell(sums)
    put(2, spread(average(sums, field2)).T)
    for x in range(SIDE):
        base = LANES * (x % 4)
        out_ref[PLANE * x : PLANE * (x + 1), :] = plane[2, x // 4, :, base : base + 20]

    for copy in halo_copies1 + move_copies1 + halo_copies2 + move_copies2:
        copy.wait_send()


def shards(
    sizes,
    scalars,
    particle_mass,
    cell_first,
    cell_second,
    cell_final,
    offset_first,
    offset_second,
    face_first,
    face_second,
    mean_field,
    mix_rate,
    react_in,
    hidden_bias,
    react_out,
):
    row = lambda a: a.reshape(1, -1)
    operands = [
        scalars,
        row(particle_mass),
        row(cell_first),
        row(cell_second),
        row(cell_final),
        offset_first,
        offset_second,
        row(face_first),
        row(face_second),
        mean_field.transpose(1, 2, 3, 0).reshape(SIDE * PLANE, 20),
        mix_rate.reshape(PLANE, SIDE),
        react_in.T,
        row(hidden_bias),
        react_out,
    ]
    operands = [pltpu.with_memory_space_constraint(a, pltpu.HBM) for a in operands]
    vmem = pl.BlockSpec(memory_space=pltpu.VMEM)
    result = pl.pallas_call(
        functools.partial(kernel, sizes),
        out_shape=jax.ShapeDtypeStruct((SIDE * PLANE, 20), F32),
        in_specs=[pl.BlockSpec(memory_space=pltpu.HBM)] * len(operands),
        out_specs=vmem,
        scratch_shapes=[pltpu.VMEM(a.shape, a.dtype) for a in operands]
        + [
            pltpu.VMEM((3, 2, PLANE, 128), F32),
            pltpu.VMEM((2, 2, 2, SIDE, 128), F32),
            pltpu.VMEM((2, 4, 2, 1, 128), F32),
            pltpu.VMEM((2, 2, ROWS, 128), F32),
            pltpu.VMEM((2, 4, 2, SIDE, 128), F32),
            pltpu.VMEM((2, 4, 2, 1, 128), F32),
            pltpu.VMEM((2, 2, 4, SIDE, 128), F32),
            pltpu.VMEM((2, 2, 4, 1, 128), F32),
            pltpu.VMEM((2, 2, ROWS, 128), F32),
            pltpu.VMEM((2, 6, 16, 128), F32),
            pltpu.VMEM((2, 6, 16, 128), F32),
            pltpu.VMEM((2, ROWS, 128), F32),
            pltpu.VMEM((32, 1024), F32),
            pltpu.SemaphoreType.DMA((INPUTS,)),
            pltpu.SemaphoreType.DMA((2, 26)),
            pltpu.SemaphoreType.DMA((2, 26)),
            pltpu.SemaphoreType.DMA((2, 6)),
            pltpu.SemaphoreType.DMA((2, 6)),
        ],
        compiler_params=pltpu.CompilerParams(
            collective_id=0, has_side_effects=True, vmem_limit_bytes=40 * 1024 * 1024
        ),
    )(*operands)
    return result.reshape(SIDE, SIDE, SIDE, 20).transpose(3, 0, 1, 2)


def solution(mesh):
    particles = P(("gx", "gy", "gz"))
    in_specs = (
        P(None, ("gx", "gy", "gz")),
        particles,
        particles,
        particles,
        particles,
        P(None, ("gx", "gy", "gz")),
        P(None, ("gx", "gy", "gz")),
        particles,
        particles,
        P(None, "gx", "gy", "gz"),
        P("gx", "gy", "gz"),
        P(),
        P(),
        P(),
    )
    sizes = (mesh.shape["gx"], mesh.shape["gy"], mesh.shape["gz"])
    return jax.shard_map(
        functools.partial(shards, sizes),
        mesh=mesh,
        in_specs=in_specs,
        out_specs=P(None, "gx", "gy", "gz"),
        check_vma=False,
    )
```

```python
import functools

import jax
import jax.numpy as jnp
from jax import lax
from jax.experimental import pallas as pl
from jax.experimental.pallas import tpu as pltpu
from jax.sharding import PartitionSpec as P

MESH = pl.DeviceIdType.MESH
F32 = jnp.float32
BF16 = jnp.bfloat16

IEM_FACTOR = 0.4
TIME_STEP = 0.4
PRIOR_MASS = 2.0

ROWS = 24
LANES = 32
SIDE = 8
PLANE = 64
BLOCK = 64

NAMES = [
    "scalars",
    "particle_mass",
    "cell_first",
    "cell_second",
    "cell_final",
    "offset_first",
    "offset_second",
    "face_first",
    "face_second",
    "mean_field",
    "mix_rate",
    "react_in",
    "hidden_bias",
    "react_out",
]
INPUTS = len(NAMES)
ORDER = ["mean_field", "mix_rate", "cell_first", "offset_first", "react_in", "hidden_bias"]
ORDER += ["react_out", "face_first", "face_second", "cell_second", "cell_final"]
ORDER += ["particle_mass", "offset_second", "scalars"]

MOVE_STEPS = [(1, 0, 0), (-1, 0, 0), (0, 0, 1), (0, 0, -1), (0, 1, 0), (0, -1, 0)]

OWN = [slice(i, i + 256) for i in range(0, 1024, 256)]
NEAR, FAR = slice(0, 256), slice(256, 384)

NT = (((1,), (1,)), ((), ()))


def dot(a, b):
    return jnp.dot(a, b, preferred_element_type=F32)


def dot_nt(a, b):
    return lax.dot_general(a, b, NT, preferred_element_type=F32)


def parts(v):
    high = v.astype(BF16)
    return high, (v - high.astype(F32)).astype(BF16)


def parts_wide(v):
    high = v.astype(BF16).astype(F32)
    return high, v - high


def iota(shape, dim):
    return lax.broadcasted_iota(jnp.int32, shape, dim)


def spline(u):
    return 0.5 * (0.5 - u) ** 2, 0.75 - u * u, 0.5 * (0.5 + u) ** 2


def along(cell, offset, low_ok, high_ok):
    low, mid, high = spline(offset)
    away = iota((SIDE, cell.shape[1]), 0) - cell
    inner = jnp.where(
        away == 0, mid, jnp.where(away == 1, high, jnp.where(away == -1, low, 0.0))
    )
    return (
        inner,
        jnp.where(cell == 0, low, 0.0) * low_ok,
        jnp.where(cell == SIDE - 1, high, 0.0) * high_ok,
    )


def weights(cells, offsets, ok):
    x_in, x_low, x_high = along(cells >> 6, offsets[0], ok[0], ok[1])
    y_in, y_low, y_high = along((cells >> 3) & 7, offsets[1], ok[2], ok[3])
    z_in, z_low, z_high = along(cells & 7, offsets[2], 1.0, 1.0)
    inner = jnp.concatenate([z_in * y_in[y : y + 1] for y in range(SIDE)], axis=0)
    row = iota(z_in.shape, 0)
    corner = jnp.where(
        row == 0,
        y_low * z_low,
        jnp.where(
            row == 1,
            y_low * z_high,
            jnp.where(row == 2, y_high * z_low, jnp.where(row == 3, y_high * z_high, 0.0)),
        ),
    )
    outer = jnp.concatenate(
        [z_in * y_low, z_in * y_high, y_in * z_low, y_in * z_high, corner, jnp.zeros_like(corner)],
        axis=0,
    )
    none = jnp.zeros((PLANE - outer.shape[0], cells.shape[1]), BF16)
    high, low = parts(outer)
    outer = jnp.concatenate([high, none, high, none, low, none], axis=0)
    return three_parts(*parts(inner)), outer, x_in, x_low, x_high


def compact(field):
    return jnp.concatenate([field[LANES * x : LANES * x + ROWS] for x in range(SIDE)], axis=0)


def spread(field):
    none = jnp.zeros((LANES - ROWS, field.shape[1]), field.dtype)
    pieces = []
    for x in range(SIDE):
        pieces += [field[ROWS * x : ROWS * (x + 1)], none]
    return jnp.concatenate(pieces, axis=0)


def three_parts(high, low):
    return jnp.concatenate([high, high, low], axis=0)


def left_of(field):
    high, low = parts_wide(field)
    return jnp.concatenate([high, low, high], axis=1).astype(BF16)


def left_outer(outer):
    high, low = parts_wide(outer)
    turned = jnp.concatenate([high, low], axis=0).T[: (SIDE + 2) * ROWS]
    return jnp.concatenate([turned, turned[:, :PLANE]], axis=1).astype(BF16)


def gather_own(result, x_in):
    total = x_in[0:1] * result[:ROWS]
    for x in range(1, SIDE):
        total = total + x_in[x : x + 1] * result[ROWS * x : ROWS * (x + 1)]
    return total


def gather(left, ws, which):
    results = [dot(left, w[which]) for w in ws]
    totals = []
    for result, w in zip(results, ws):
        sides = result[SIDE * ROWS :]
        own = gather_own(result, w[2])
        totals.append(own + w[3] * sides[:ROWS] + w[4] * sides[ROWS:])
    return totals


def mix(values, sampled):
    mixed = values - IEM_FACTOR * sampled[20:21] * (values - sampled)
    return jnp.where(iota(mixed.shape, 0) == 20, 1.0, mixed)


def first_operand(mixed):
    high, low = parts_wide(mixed)
    none = jnp.zeros((128 - 3 * ROWS, mixed.shape[1]), F32)
    return jnp.concatenate([high, low, high, none], axis=0).astype(BF16)


def react(values, sampled, first, second):
    mixed = [mix(one, sample) for one, sample in zip(values, sampled)]
    operands = [first_operand(one) for one in mixed]
    hidden = [dot(first, one) for one in operands]
    hidden = [jnp.concatenate(parts(jnp.tanh(one)), axis=0) for one in hidden]
    results = [dot(second, one) for one in hidden]
    return [one + TIME_STEP * (result[:ROWS] + result[ROWS:]) for one, result in zip(mixed, results)]


def slots_of(faces):
    count = faces.shape[1]
    code = iota((SIDE, count), 0)
    own_code = jnp.where(code < 2, code + 1, jnp.where(code < 4, code + 3, code - 1))
    chosen = (own_code == faces) & (code < 6)
    mask = jnp.where(chosen, 1.0, 0.0)
    chunks = count // 128
    stacked = jnp.concatenate(
        [mask[:, 128 * j : 128 * (j + 1)] for j in range(chunks)], axis=0
    ).astype(BF16)
    row, col = iota((128, 256), 0), iota((128, 256), 1)
    counter = jnp.where((row < col) | (col >= 128), 1.0, 0.0).astype(BF16)
    ranks = dot(stacked, counter)
    before = jnp.zeros((SIDE, 128), F32)
    pieces = []
    for j in range(chunks):
        rows = slice(SIDE * j, SIDE * (j + 1))
        pieces.append(ranks[rows, :128] + before)
        before = before + ranks[rows, 128:]
    rank = jnp.concatenate(pieces, axis=1)
    place = jnp.where(chosen, rank.astype(jnp.int32) + BLOCK * code + 1, 0)
    return jnp.sum(place, axis=0, keepdims=True) - 1


def one_hot(index, size):
    shape = (16, index.shape[1])
    away = iota(shape, 0).astype(F32).astype(BF16)
    away = away - jnp.broadcast_to(index.astype(F32), shape).astype(BF16)
    one, zero = jnp.ones(shape, BF16), jnp.zeros(shape, BF16)
    return jnp.concatenate(
        [jnp.where(away == jnp.full(shape, -16.0 * b, BF16), one, zero) for b in range(size // 16)],
        axis=0,
    )


def pack_operand(payload):
    return jnp.concatenate(parts_wide(payload), axis=0).astype(BF16)


def slots_hot(slots):
    return jnp.concatenate([one_hot(slots, 256), one_hot(slots - 256, 128)], axis=0)


def scatter_operand(values, masses, cells):
    high, low = parts_wide(values * masses)
    stacked = jnp.concatenate([high, low], axis=0)
    upper = (cells >> 8).astype(F32)
    return jnp.concatenate([stacked * (1.0 - upper), stacked * upper], axis=0).astype(BF16)


def scatter(group):
    hot = [one_hot(cells & 255, 4 * PLANE) for _, _, cells in group]
    left = [scatter_operand(*one) for one in group]
    return sum(dot_nt(a, b) for a, b in zip(left, hot))


def by_cell(result):
    pieces = []
    for x in range(SIDE):
        base = 2 * ROWS * (x // 4)
        lanes = slice(PLANE * (x % 4), PLANE * (x % 4 + 1))
        pieces.append(result[base : base + ROWS, lanes] + result[base + ROWS : base + 2 * ROWS, lanes])
    return jnp.concatenate(pieces, axis=0)


def average(sums, field):
    pieces = []
    for x in range(SIDE):
        rows = slice(ROWS * x, ROWS * (x + 1))
        one, old = sums[rows], field[rows]
        new = (one + PRIOR_MASS * old) / (one[20:21] + PRIOR_MASS)
        pieces.append(jnp.where(iota(new.shape, 0) == 20, old, new))
    return jnp.concatenate(pieces, axis=0)


def kernel(sizes, *refs):
    inputs, out_ref, refs = refs[:INPUTS], refs[INPUTS], refs[INPUTS + 1 :]
    local, refs = refs[:INPUTS], refs[INPUTS:]
    (
        plane,
        z_send,
        c_send,
        x_send,
        near_got,
        tile_got,
        row_got,
        x_got,
        packed,
        got,
        rows_buf,
        pay,
        local_sem,
        halo_send_sem,
        halo_recv_sem,
        move_send_sem,
        move_recv_sem,
    ) = refs
    n_gx, n_gy, n_gz = sizes
    gx, gy, gz = lax.axis_index("gx"), lax.axis_index("gy"), lax.axis_index("gz")

    def three(index, size):
        return {-1: lax.rem(index + size - 1, size), 0: index, 1: lax.rem(index + 1, size)}

    near_x, near_y, near_z = three(gx, n_gx), three(gy, n_gy), three(gz, n_gz)

    def at(dx, dy, dz):
        return near_x[dx], near_y[dy], near_z[dz]

    signs = (1, -1)
    y_steps = [(0, dy, 0) for dy in signs]
    near_steps = [(dx, 0, dz) for dz in signs for dx in signs]
    near_steps += [(0, 0, dz) for dz in signs]
    x_steps = [(dx, 0, 0) for dx in signs]
    halo_steps = near_steps + x_steps + y_steps

    barrier = pltpu.get_barrier_semaphore()
    for step in halo_steps:
        pl.semaphore_signal(barrier, inc=1, device_id=at(*step), device_id_type=MESH)
    loads = {
        name: pltpu.make_async_copy(a, to, local_sem.at[i])
        for i, (name, a, to) in enumerate(zip(NAMES, inputs, local))
    }
    for name in ORDER:
        loads[name].start()

    def load(name):
        loads[name].wait()
        return local[NAMES.index(name)]

    def remote_copy(src, dst, send_sem, recv_sem, step):
        return pltpu.make_async_remote_copy(
            src_ref=src,
            dst_ref=dst,
            send_sem=send_sem,
            recv_sem=recv_sem,
            device_id=at(*step),
            device_id_type=MESH,
        )

    def put(h, value):
        plane[h, 0] = value[:, :128]
        plane[h, 1] = value[:, 128:]

    def all_of(buffer, send_sem, recv_sem):
        return remote_copy(buffer, buffer, send_sem, recv_sem, (1, 0, 0))

    def halo_kind(h, kind):
        buffer = (x_got, near_got, tile_got, row_got)[kind].at[h]
        return all_of(buffer, halo_send_sem.at[h, kind], halo_recv_sem.at[h, kind])

    def send_halo(h, kind, steps, source, target):
        for step, src, dst in zip(steps, source, target):
            remote_copy(
                src, dst, halo_send_sem.at[h, kind], halo_recv_sem.at[h, kind], step
            ).start()

    def prepare_near(h, field):
        x_send[h, 0, :, 0:PLANE] = field[7 * ROWS : 8 * ROWS]
        x_send[h, 1, :, 0:PLANE] = field[0:ROWS]
        put(h, jnp.concatenate([field, jnp.zeros((64, PLANE), F32)], axis=0).T)
        for z, slot in ((7, 0), (0, 1)):
            for half in range(2):
                z_send[h, slot, half] = plane[h, half, pl.ds(z, SIDE, stride=SIDE), :]

    def send_near(h):
        source = [z_send.at[h, slot, half] for slot in range(2) for half in (1, 0)]
        target = [near_got.at[h, 4 + 2 * slot + k] for slot in range(2) for k in range(2)]
        source += [z_send.at[h, slot] for slot in range(2)]
        target += [near_got.at[h, 2 * slot : 2 * slot + 2] for slot in range(2)]
        send_halo(h, 1, near_steps, source, target)
        send_halo(h, 0, x_steps, [x_send.at[h, k] for k in range(2)], [x_got.at[h, k] for k in range(2)])

    def send_y(h, field):
        halo_kind(h, 0).wait_recv()
        sides = jnp.concatenate([x_got[h, 0], x_got[h, 1]], axis=0)[:, :PLANE]
        put(h + 2, jnp.concatenate([field, sides, jnp.zeros((16, PLANE), F32)], axis=0).T)
        rows = plane.at[h + 2]
        y_rows = (slice(56, 64), slice(0, 8))
        send_halo(h, 2, y_steps, [rows.at[:, y] for y in y_rows], [tile_got.at[h, k] for k in range(2)])
        halo_kind(h, 1).wait_recv()
        lane = iota((SIDE, 128), 1)
        outer = []
        for slot in range(2):
            low = pltpu.roll(near_got[h, 4 + 2 * slot], 24, 1)
            high = pltpu.roll(near_got[h, 5 + 2 * slot], 88, 1)
            second_half = jnp.where(
                lane < 64, near_got[h, 2 * slot + 1], jnp.where(lane < 88, low, high)
            )
            halves = (near_got[h, 2 * slot], second_half)
            outer.append(jnp.concatenate(halves, axis=1))
            for half in range(2):
                c_send[h, 0, 2 * slot + half] = halves[half][7:8]
                c_send[h, 1, 2 * slot + half] = halves[half][0:1]
        send_halo(h, 3, y_steps, [c_send.at[h, k] for k in range(2)], [row_got.at[h, k] for k in range(2)])
        return jnp.concatenate([left_of(field), left_of(sides)], axis=0), outer

    def outer_left(h, outer):
        for kind in (2, 3):
            halo_kind(h, kind).wait_recv()
        faces = [jnp.concatenate([tile_got[h, k, 0], tile_got[h, k, 1]], axis=1) for k in range(2)]
        row = iota((SIDE, 256), 0)
        last = jnp.zeros((SIDE, 256), F32)
        for k in range(2):
            for slot in range(2):
                one = [row_got[h, k, 2 * slot + half] for half in range(2)]
                last = jnp.where(row == 2 * k + slot, jnp.concatenate(one, axis=1), last)
        none = jnp.zeros((PLANE - 5 * SIDE, 256), F32)
        return left_outer(jnp.concatenate(faces + outer + [last, none], axis=0))

    lower = iota((16, 128), 1) < BLOCK

    def turned(value):
        return pltpu.roll(value, BLOCK, 1)

    def move_sems(m, first):
        return move_send_sem.at[m, first // 4], move_recv_sem.at[m, first // 4]

    def moves(m, first):
        return all_of(got.at[m, 4:6] if first else got.at[m, 0:4], *move_sems(m, first))

    def send_moves(m, first, block):
        for t in range(block.shape[1] // 128):
            tile = block[:, 128 * t : 128 * (t + 1)]
            k = first + 2 * t
            packed[m, k] = jnp.where(lower, tile[:16], turned(tile[16:]))
            packed[m, k + 1] = jnp.where(lower, turned(tile[:16]), tile[16:])
            for i in (k, k + 1):
                remote_copy(
                    packed.at[m, i], got.at[m, i], *move_sems(m, first), MOVE_STEPS[i]
                ).start()

    def arrivals(m, first):
        moves(m, first).wait_recv()
        tiles = []
        for k in (4,) if first else (0, 2):
            one, two = got[m, k], got[m, k + 1]
            top = jnp.where(lower, one, turned(two))
            bottom = jnp.where(lower, turned(one), two)
            tiles.append(jnp.concatenate([top, bottom], axis=0))
        return jnp.concatenate(tiles, axis=1)

    def sent(h):
        for kind in range(4):
            halo_kind(h, kind).wait_send()

    plane[0] = jnp.zeros((2, PLANE, 128), F32)
    x_send[...] = jnp.zeros(x_send.shape, F32)
    same_z = jnp.where(iota((PLANE, SIDE), 0) & 7 == iota((PLANE, SIDE), 1), 1.0, 0.0)
    same_y = iota((PLANE, PLANE), 0) >> 3 == iota((PLANE, PLANE), 1) & 7
    goes = (iota((PLANE, SIDE * LANES), 0) >> 3) * LANES + 20
    goes = jnp.where(iota((PLANE, SIDE * LANES), 1) == goes, 1.0, 0.0).astype(BF16)
    rate = jnp.zeros((PLANE, SIDE * LANES), F32)
    for part in parts(load("mix_rate")[...]):
        along_z = jnp.where(same_y, dot_nt(same_z.astype(BF16), part), 0.0)
        rate = rate + dot(along_z.astype(BF16), goes)
    mean_ref = load("mean_field")
    for x in range(SIDE):
        base = LANES * (x % 4)
        plane[0, x // 4, :, base : base + 20] = mean_ref[PLANE * x : PLANE * (x + 1), :]
    field1 = compact((jnp.concatenate([plane[0, 0], plane[0, 1]], axis=1) + rate).T)
    prepare_near(0, field1)

    pl.semaphore_wait(barrier, len(halo_steps))
    send_near(0)

    ok = [
        jnp.where(gx > 0, 1.0, 0.0),
        jnp.where(gx < n_gx - 1, 1.0, 0.0),
        jnp.where(gy > 0, 1.0, 0.0),
        jnp.where(gy < n_gy - 1, 1.0, 0.0),
    ]

    cell1 = load("cell_first")
    off1 = load("offset_first")
    face1 = load("face_first")
    cell2 = load("cell_second")
    cell3 = load("cell_final")
    mass = load("particle_mass")
    off2 = load("offset_second")
    pay[0:20, :] = load("scalars")[...]
    pay[20:21, :] = mass[...]
    pay[21:24, :] = off2[...]
    pay[24:25, :] = cell2[...].astype(F32)
    pay[25:26, :] = cell3[...].astype(F32)
    pay[26:27, :] = cell1[...].astype(F32)
    pay[27:30, :] = off1[...]
    pay[30:32, :] = jnp.zeros((2, pay.shape[1]), F32)

    def packed_movers(faces):
        slots = slots_of(faces)
        hot = [slots_hot(slots[:, lanes]) for lanes in OWN]
        left = [pack_operand(pay[:, lanes]) for lanes in OWN]
        block = sum(dot_nt(a, b) for a, b in zip(left, hot))
        return block[:32] + block[32:]

    def weights_at(cells, offsets, lanes):
        return weights(cells[:, lanes], [offsets[d : d + 1, lanes] for d in range(3)], ok)

    def scalars_of(block):
        row = iota((ROWS, block.shape[1]), 0)
        return jnp.where(row == 20, 1.0, jnp.where(row < 20, block[:ROWS], 0.0))

    def message(values, block):
        row = iota((ROWS, block.shape[1]), 0)
        return jnp.concatenate([jnp.where(row < 20, values, block[:ROWS]), block[ROWS:]], axis=0)

    def work(values, sampled, outer, ws):
        more = gather(outer, ws, 1)
        return react(values, [a + b for a, b in zip(sampled, more)], first, second)

    def work_movers(m, movers, inner, outer, ws):
        blocks = [movers[:, lanes] for lanes in (FAR, NEAR)]
        new = work([scalars_of(block) for block in blocks], inner, outer, ws)
        messages = [message(one, block) for one, block in zip(new, blocks)]
        for first, one in zip((4, 0), messages):
            send_moves(m, first, one)

    movers = packed_movers(face1[...])
    mover_cells = movers[26:27].astype(jnp.int32)
    w_movers = [weights_at(mover_cells, movers[27:30], lanes) for lanes in (FAR, NEAR)]

    rows_buf[...] = jnp.zeros(rows_buf.shape, F32)
    rows_buf[0, 0:20, :] = load("react_in")[...]
    rows_buf[0, 20:21, :] = load("hidden_bias")[...]
    rows_buf[1, 0:20, :] = load("react_out")[...]
    high, low = parts_wide(rows_buf[0])
    first = jnp.concatenate(
        [high, high, low, jnp.zeros((128 - 3 * ROWS, 128), F32)], axis=0
    ).T.astype(BF16)
    high, low = parts_wide(rows_buf[1])
    second = jnp.concatenate(
        [
            jnp.concatenate([high, high], axis=1),
            jnp.concatenate([low, jnp.zeros_like(low)], axis=1),
        ],
        axis=0,
    ).astype(BF16)

    left, outer = send_y(0, field1)
    in_movers = gather(left, w_movers, 0)
    w_own = [weights_at(cell1, off1, lanes) for lanes in OWN]
    in_own = gather(left, w_own, 0)

    outer = outer_left(0, outer)
    work_movers(0, movers, in_movers, outer, w_movers)

    values = work([scalars_of(pay[:, lanes]) for lanes in OWN], in_own, outer, w_own)
    stay = [jnp.where(face1[:, lanes] == 0, mass[:, lanes], 0.0) for lanes in OWN]
    sums = scatter([(v, m, cell2[:, lanes]) for v, m, lanes in zip(values, stay, OWN)])
    for one, lanes in zip(values, OWN):
        pay[0:20, lanes] = one[:20]

    lane = iota((1, 128), 1)
    alive = {
        0: jnp.concatenate([jnp.where(lane < 64, ok[0], ok[1]), jnp.ones((1, 128), F32)], axis=1),
        4: jnp.where(lane < 64, ok[2], ok[3]),
    }

    came = {}
    for i in (0, 4):
        block = arrivals(0, i)
        came[i] = block
        cells = block[24:25].astype(jnp.int32)
        sums = sums + scatter([(scalars_of(block), block[20:21] * alive[i], cells)])
    field2 = average(by_cell(sums), field1)
    prepare_near(1, field2)
    send_near(1)

    face2 = load("face_second")
    movers = packed_movers(face2[...])
    mover_cells = movers[24:25].astype(jnp.int32)
    w_movers = [weights_at(mover_cells, movers[21:24], lanes) for lanes in (FAR, NEAR)]
    left, outer = send_y(1, field2)
    in_movers = gather(left, w_movers, 0)
    w_own = [weights_at(cell2, off2, lanes) for lanes in OWN]
    w_own += [
        weights_at(block[24:25].astype(jnp.int32), block[21:24], slice(None))
        for block in came.values()
    ]
    in_own = gather(left, w_own, 0)

    outer = outer_left(1, outer)
    work_movers(1, movers, in_movers, outer, w_movers)

    values = work(values + [scalars_of(block) for block in came.values()], in_own, outer, w_own)
    masses = [
        jnp.where(face1[:, lanes] + face2[:, lanes] == 0, mass[:, lanes], 0.0) for lanes in OWN
    ] + [block[20:21] * alive[i] for i, block in came.items()]
    cells = [cell3[:, lanes] for lanes in OWN]
    cells += [block[25:26].astype(jnp.int32) for block in came.values()]
    sums = scatter(list(zip(values, masses, cells)))

    sent(0)
    sent(1)
    for i in (0, 4):
        moves(0, i).wait_send()

    for i in (0, 4):
        block = arrivals(1, i)
        cells = block[25:26].astype(jnp.int32)
        sums = sums + scatter([(scalars_of(block), block[20:21] * alive[i], cells)])
    sums = by_cell(sums)
    put(4, spread(average(sums, field2)).T)
    for x in range(SIDE):
        base = LANES * (x % 4)
        out_ref[PLANE * x : PLANE * (x + 1), :] = plane[4, x // 4, :, base : base + 20]

    for i in (0, 4):
        moves(1, i).wait_send()


def shards(
    sizes,
    scalars,
    particle_mass,
    cell_first,
    cell_second,
    cell_final,
    offset_first,
    offset_second,
    face_first,
    face_second,
    mean_field,
    mix_rate,
    react_in,
    hidden_bias,
    react_out,
):
    row = lambda a: a.reshape(1, -1)
    operands = [
        scalars,
        row(particle_mass),
        row(cell_first),
        row(cell_second),
        row(cell_final),
        offset_first,
        offset_second,
        row(face_first),
        row(face_second),
        mean_field.transpose(1, 2, 3, 0).reshape(SIDE * PLANE, 20),
        mix_rate.reshape(PLANE, SIDE),
        react_in.T,
        row(hidden_bias),
        react_out,
    ]
    operands = [pltpu.with_memory_space_constraint(a, pltpu.HBM) for a in operands]
    vmem = pl.BlockSpec(memory_space=pltpu.VMEM)
    result = pl.pallas_call(
        functools.partial(kernel, sizes),
        out_shape=jax.ShapeDtypeStruct((SIDE * PLANE, 20), F32),
        in_specs=[pl.BlockSpec(memory_space=pltpu.HBM)] * len(operands),
        out_specs=vmem,
        scratch_shapes=[pltpu.VMEM(a.shape, a.dtype) for a in operands]
        + [
            pltpu.VMEM((5, 2, PLANE, 128), F32),
            pltpu.VMEM((2, 2, 2, SIDE, 128), F32),
            pltpu.VMEM((2, 2, 4, 1, 128), F32),
            pltpu.VMEM((2, 2, ROWS, 128), F32),
            pltpu.VMEM((2, 8, SIDE, 128), F32),
            pltpu.VMEM((2, 2, 2, SIDE, 128), F32),
            pltpu.VMEM((2, 2, 4, 1, 128), F32),
            pltpu.VMEM((2, 2, ROWS, 128), F32),
            pltpu.VMEM((2, 6, 16, 128), F32),
            pltpu.VMEM((2, 6, 16, 128), F32),
            pltpu.VMEM((2, ROWS, 128), F32),
            pltpu.VMEM((32, 1024), F32),
            pltpu.SemaphoreType.DMA((INPUTS,)),
            pltpu.SemaphoreType.DMA((2, 4)),
            pltpu.SemaphoreType.DMA((2, 4)),
            pltpu.SemaphoreType.DMA((2, 2)),
            pltpu.SemaphoreType.DMA((2, 2)),
        ],
        compiler_params=pltpu.CompilerParams(
            collective_id=0, has_side_effects=True, vmem_limit_bytes=40 * 1024 * 1024
        ),
    )(*operands)
    return result.reshape(SIDE, SIDE, SIDE, 20).transpose(3, 0, 1, 2)


def solution(mesh):
    particles = P(("gx", "gy", "gz"))
    in_specs = (
        P(None, ("gx", "gy", "gz")),
        particles,
        particles,
        particles,
        particles,
        P(None, ("gx", "gy", "gz")),
        P(None, ("gx", "gy", "gz")),
        particles,
        particles,
        P(None, "gx", "gy", "gz"),
        P("gx", "gy", "gz"),
        P(),
        P(),
        P(),
    )
    sizes = (mesh.shape["gx"], mesh.shape["gy"], mesh.shape["gz"])
    return jax.shard_map(
        functools.partial(shards, sizes),
        mesh=mesh,
        in_specs=in_specs,
        out_specs=P(None, "gx", "gy", "gz"),
        check_vma=False,
    )
```

```python
import functools

import jax
import jax.numpy as jnp
from jax import lax
from jax.experimental import pallas as pl
from jax.experimental.pallas import tpu as pltpu
from jax.sharding import PartitionSpec as P

MESH = pl.DeviceIdType.MESH
F32 = jnp.float32
BF16 = jnp.bfloat16

IEM_FACTOR = 0.4
TIME_STEP = 0.4
PRIOR_MASS = 2.0

ROWS = 24
LANES = 32
SIDE = 8
PLANE = 64
BLOCK = 64

NAMES = [
    "scalars",
    "particle_mass",
    "cell_first",
    "cell_second",
    "cell_final",
    "offset_first",
    "offset_second",
    "face_first",
    "face_second",
    "mean_field",
    "mix_rate",
    "react_in",
    "hidden_bias",
    "react_out",
]
INPUTS = len(NAMES)
ORDER = ["mean_field", "mix_rate", "cell_first", "offset_first", "react_in", "hidden_bias"]
ORDER += ["react_out", "face_first", "face_second", "cell_second", "cell_final"]
ORDER += ["particle_mass", "offset_second", "scalars"]

MOVE_STEPS = [(1, 0, 0), (-1, 0, 0), (0, 0, 1), (0, 0, -1), (0, 1, 0), (0, -1, 0)]

OWN = [slice(i, i + 256) for i in range(0, 1024, 256)]
NEAR, FAR = slice(0, 256), slice(256, 384)

NT = (((1,), (1,)), ((), ()))


def dot(a, b):
    return jnp.dot(a, b, preferred_element_type=F32)


def dot_nt(a, b):
    return lax.dot_general(a, b, NT, preferred_element_type=F32)


def parts(v):
    high = v.astype(BF16)
    return high, (v - high.astype(F32)).astype(BF16)


def parts_wide(v):
    high = v.astype(BF16).astype(F32)
    return high, v - high


def iota(shape, dim):
    return lax.broadcasted_iota(jnp.int32, shape, dim)


def spline(u):
    return 0.5 * (0.5 - u) ** 2, 0.75 - u * u, 0.5 * (0.5 + u) ** 2


def along(cell, offset, low_ok, high_ok):
    low, mid, high = spline(offset)
    away = iota((SIDE, cell.shape[1]), 0) - cell
    inner = jnp.where(
        away == 0, mid, jnp.where(away == 1, high, jnp.where(away == -1, low, 0.0))
    )
    return (
        inner,
        jnp.where(cell == 0, low, 0.0) * low_ok,
        jnp.where(cell == SIDE - 1, high, 0.0) * high_ok,
    )


def weights(cells, offsets, ok):
    x_in, x_low, x_high = along(cells >> 6, offsets[0], ok[0], ok[1])
    y_in, y_low, y_high = along((cells >> 3) & 7, offsets[1], ok[2], ok[3])
    z_in, z_low, z_high = along(cells & 7, offsets[2], 1.0, 1.0)
    inner = jnp.concatenate([z_in * y_in[y : y + 1] for y in range(SIDE)], axis=0)
    row = iota(z_in.shape, 0)
    corner = jnp.where(
        row == 0,
        y_low * z_low,
        jnp.where(
            row == 1,
            y_low * z_high,
            jnp.where(row == 2, y_high * z_low, jnp.where(row == 3, y_high * z_high, 0.0)),
        ),
    )
    outer = jnp.concatenate(
        [z_in * y_low, z_in * y_high, y_in * z_low, y_in * z_high, corner, jnp.zeros_like(corner)],
        axis=0,
    )
    none = jnp.zeros((PLANE - outer.shape[0], cells.shape[1]), BF16)
    high, low = parts(outer)
    outer = jnp.concatenate([high, none, high, none, low, none], axis=0)
    return three_parts(*parts(inner)), outer, x_in, x_low, x_high


def compact(field):
    return jnp.concatenate([field[LANES * x : LANES * x + ROWS] for x in range(SIDE)], axis=0)


def spread(field):
    none = jnp.zeros((LANES - ROWS, field.shape[1]), field.dtype)
    pieces = []
    for x in range(SIDE):
        pieces += [field[ROWS * x : ROWS * (x + 1)], none]
    return jnp.concatenate(pieces, axis=0)


def three_parts(high, low):
    return jnp.concatenate([high, high, low], axis=0)


def left_of(field):
    high, low = parts_wide(field)
    return jnp.concatenate([high, low, high], axis=1).astype(BF16)


def left_outer(outer):
    high, low = parts_wide(outer)
    turned = jnp.concatenate([high, low], axis=0).T
    base = SIDE * LANES
    rows = jnp.concatenate(
        [
            compact(turned[:base]),
            turned[base + 3 * LANES : base + 3 * LANES + ROWS],
            turned[base : base + ROWS],
        ],
        axis=0,
    )
    return jnp.concatenate([rows, rows[:, :PLANE]], axis=1).astype(BF16)


def gather_own(result, x_in):
    total = x_in[0:1] * result[:ROWS]
    for x in range(1, SIDE):
        total = total + x_in[x : x + 1] * result[ROWS * x : ROWS * (x + 1)]
    return total


def gather(left, ws, which):
    results = [dot(left, w[which]) for w in ws]
    totals = []
    for result, w in zip(results, ws):
        sides = result[SIDE * ROWS :]
        own = gather_own(result, w[2])
        totals.append(own + w[3] * sides[:ROWS] + w[4] * sides[ROWS:])
    return totals


def mix(values, sampled):
    mixed = values - IEM_FACTOR * sampled[20:21] * (values - sampled)
    return jnp.where(iota(mixed.shape, 0) == 20, 1.0, mixed)


def first_operand(mixed):
    high, low = parts_wide(mixed)
    none = jnp.zeros((128 - 3 * ROWS, mixed.shape[1]), F32)
    return jnp.concatenate([high, low, high, none], axis=0).astype(BF16)


def react(values, sampled, first, second):
    mixed = [mix(one, sample) for one, sample in zip(values, sampled)]
    operands = [first_operand(one) for one in mixed]
    hidden = [dot(first, one) for one in operands]
    hidden = [jnp.concatenate(parts(jnp.tanh(one)), axis=0) for one in hidden]
    results = [dot(second, one) for one in hidden]
    return [one + TIME_STEP * (result[:ROWS] + result[ROWS:]) for one, result in zip(mixed, results)]


def slots_of(faces):
    count = faces.shape[1]
    code = iota((SIDE, count), 0)
    own_code = jnp.where(code < 2, code + 1, jnp.where(code < 4, code + 3, code - 1))
    chosen = (own_code == faces) & (code < 6)
    mask = jnp.where(chosen, 1.0, 0.0)
    chunks = count // 128
    stacked = jnp.concatenate(
        [mask[:, 128 * j : 128 * (j + 1)] for j in range(chunks)], axis=0
    ).astype(BF16)
    row, col = iota((128, 256), 0), iota((128, 256), 1)
    counter = jnp.where((row < col) | (col >= 128), 1.0, 0.0).astype(BF16)
    ranks = dot(stacked, counter)
    before = jnp.zeros((SIDE, 128), F32)
    pieces = []
    for j in range(chunks):
        rows = slice(SIDE * j, SIDE * (j + 1))
        pieces.append(ranks[rows, :128] + before)
        before = before + ranks[rows, 128:]
    rank = jnp.concatenate(pieces, axis=1)
    place = jnp.where(chosen, rank.astype(jnp.int32) + BLOCK * code + 1, 0)
    return jnp.sum(place, axis=0, keepdims=True) - 1


def one_hot(index, size):
    shape = (16, index.shape[1])
    away = iota(shape, 0).astype(F32).astype(BF16)
    away = away - jnp.broadcast_to(index.astype(F32), shape).astype(BF16)
    one, zero = jnp.ones(shape, BF16), jnp.zeros(shape, BF16)
    return jnp.concatenate(
        [jnp.where(away == jnp.full(shape, -16.0 * b, BF16), one, zero) for b in range(size // 16)],
        axis=0,
    )


def pack_operand(payload):
    return jnp.concatenate(parts_wide(payload), axis=0).astype(BF16)


def slots_hot(slots):
    return jnp.concatenate([one_hot(slots, 256), one_hot(slots - 256, 128)], axis=0)


def scatter_operand(values, masses, cells):
    high, low = parts_wide(values * masses)
    stacked = jnp.concatenate([high, low], axis=0)
    upper = (cells >> 8).astype(F32)
    return jnp.concatenate([stacked * (1.0 - upper), stacked * upper], axis=0).astype(BF16)


def scatter(group):
    hot = [one_hot(cells & 255, 4 * PLANE) for _, _, cells in group]
    left = [scatter_operand(*one) for one in group]
    return sum(dot_nt(a, b) for a, b in zip(left, hot))


def by_cell(result):
    pieces = []
    for x in range(SIDE):
        base = 2 * ROWS * (x // 4)
        lanes = slice(PLANE * (x % 4), PLANE * (x % 4 + 1))
        pieces.append(result[base : base + ROWS, lanes] + result[base + ROWS : base + 2 * ROWS, lanes])
    return jnp.concatenate(pieces, axis=0)


def average(sums, field):
    pieces = []
    for x in range(SIDE):
        rows = slice(ROWS * x, ROWS * (x + 1))
        one, old = sums[rows], field[rows]
        new = (one + PRIOR_MASS * old) / (one[20:21] + PRIOR_MASS)
        pieces.append(jnp.where(iota(new.shape, 0) == 20, old, new))
    return jnp.concatenate(pieces, axis=0)


def kernel(sizes, *refs):
    inputs, out_ref, refs = refs[:INPUTS], refs[INPUTS], refs[INPUTS + 1 :]
    local, refs = refs[:INPUTS], refs[INPUTS:]
    (
        plane,
        z_send,
        c_send,
        x_send,
        tile_got,
        row_got,
        x_got,
        packed,
        got,
        rows_buf,
        pay,
        local_sem,
        halo_send_sem,
        halo_recv_sem,
        move_send_sem,
        move_recv_sem,
    ) = refs
    n_gx, n_gy, n_gz = sizes
    gx, gy, gz = lax.axis_index("gx"), lax.axis_index("gy"), lax.axis_index("gz")

    def three(index, size):
        return {-1: lax.rem(index + size - 1, size), 0: index, 1: lax.rem(index + 1, size)}

    near_x, near_y, near_z = three(gx, n_gx), three(gy, n_gy), three(gz, n_gz)

    def at(dx, dy, dz):
        return near_x[dx], near_y[dy], near_z[dz]

    faces = [(1, 0), (-1, 0), (0, 1), (0, -1)]
    corners = [(1, 1), (1, -1), (-1, 1), (-1, -1)]
    x_steps = [1, -1]
    halo_steps = [(dx, dy, dz) for dx in x_steps for dy, dz in corners]
    halo_steps += [(0, dy, dz) for dy, dz in corners]
    halo_steps += [(dx, dy, 0) for dx in x_steps for dy in (1, -1)]
    halo_steps += [(0, dy, 0) for dy in (1, -1)]
    halo_steps += [(dx, 0, dz) for dx in x_steps for dz in (1, -1)]
    halo_steps += [(0, 0, dz) for dz in (1, -1)]
    halo_steps += [(dx, 0, 0) for dx in x_steps]

    loads = {
        name: pltpu.make_async_copy(a, to, local_sem.at[i])
        for i, (name, a, to) in enumerate(zip(NAMES, inputs, local))
    }
    barrier = pltpu.get_barrier_semaphore()
    for step in halo_steps:
        pl.semaphore_signal(barrier, inc=1, device_id=at(*step), device_id_type=MESH)
    for name in ORDER:
        loads[name].start()

    def load(name):
        loads[name].wait()
        return local[NAMES.index(name)]

    def remote_copy(src, dst, send_sem, recv_sem, step):
        return pltpu.make_async_remote_copy(
            src_ref=src,
            dst_ref=dst,
            send_sem=send_sem,
            recv_sem=recv_sem,
            device_id=at(*step),
            device_id_type=MESH,
        )

    def put(h, value):
        plane[h, 0] = value[:, :128]
        plane[h, 1] = value[:, 128:]

    def all_of(buffer, send_sem, recv_sem):
        return remote_copy(buffer, buffer, send_sem, recv_sem, (1, 0, 0))

    def halo_kind(h, kind):
        buffer = (tile_got, row_got, x_got)[kind].at[h]
        return all_of(buffer, halo_send_sem.at[h, kind], halo_recv_sem.at[h, kind])

    def send_halo(h, first, kind, source, target):
        for i, (src, dst) in enumerate(zip(source, target)):
            remote_copy(
                src, dst, halo_send_sem.at[h, kind], halo_recv_sem.at[h, kind], halo_steps[first + i]
            ).start()

    def prepare_x(h, field):
        x_send[h, 0, :, 0:PLANE] = field[7 * ROWS : 8 * ROWS]
        x_send[h, 1, :, 0:PLANE] = field[0:ROWS]

    def send_x(h):
        send_halo(h, 24, 2, [x_send.at[h, k] for k in range(2)], [x_got.at[h, k] for k in range(2)])

    def prepare_corners(h):
        for slot, row in enumerate((63, 56, 7, 0)):
            for half in range(2):
                c_send[h, slot, half] = plane[h, half, row : row + 1, :]

    def prepare_z(h):
        for z, slot in ((7, 0), (0, 1)):
            for half in range(2):
                z_send[h, slot, half] = plane[h, half, pl.ds(z, SIDE, stride=SIDE), :]

    def send_y(h):
        sides = ((0, 1), (1, 0))
        source = [c_send.at[h, slot, half] for _, half in sides for slot in range(4)]
        target = [row_got.at[h, 8 + 4 * k + slot] for k, _ in sides for slot in range(4)]
        source += [c_send.at[h, slot] for slot in range(4)]
        target += [row_got.at[h, 2 * slot : 2 * slot + 2] for slot in range(4)]
        send_halo(h, 0, 1, source, target)
        rows = plane.at[h]
        y_rows = (slice(56, 64), slice(0, 8))
        source = [rows.at[half, y] for _, half in sides for y in y_rows]
        target = [tile_got.at[h, 8 + 4 * k + slot] for k, _ in sides for slot in range(2)]
        source += [rows.at[:, y] for y in y_rows]
        target += [tile_got.at[h, 2 * slot : 2 * slot + 2] for slot in range(2)]
        send_halo(h, 12, 0, source, target)

    def send_z(h):
        sides = ((0, 1), (1, 0))
        source = [z_send.at[h, slot, half] for _, half in sides for slot in range(2)]
        target = [tile_got.at[h, 10 + 4 * k + slot] for k, _ in sides for slot in range(2)]
        source += [z_send.at[h, slot] for slot in range(2)]
        target += [tile_got.at[h, 4 + 2 * slot : 6 + 2 * slot] for slot in range(2)]
        send_halo(h, 18, 0, source, target)

    def stack_outer(face, corner):
        row = iota((SIDE, 128), 0)
        last = jnp.zeros((SIDE, 128), F32)
        for slot in range(4):
            last = jnp.where(row == slot, corner[slot], last)
        none = jnp.zeros((PLANE - 5 * SIDE, 128), F32)
        return jnp.concatenate(face + [last, none], axis=0)

    def inner_left(h, field):
        halo_kind(h, 2).wait_recv()
        sides = jnp.concatenate([x_got[h, 0], x_got[h, 1]], axis=0)[:, :PLANE]
        return jnp.concatenate([left_of(field), left_of(sides)], axis=0)

    def outer_left(h):
        for kind in range(2):
            halo_kind(h, kind).wait_recv()
        both = [
            stack_outer(
                [tile_got[h, 2 * slot + half] for slot in range(4)],
                [row_got[h, 2 * slot + half] for slot in range(4)],
            )
            for half in range(2)
        ]
        side = [
            stack_outer(
                [tile_got[h, 8 + 4 * k + slot] for slot in range(4)],
                [row_got[h, 8 + 4 * k + slot] for slot in range(4)],
            )
            for k in range(2)
        ]
        last = jnp.where(iota((PLANE, 128), 1) < PLANE, side[1], side[0])
        return left_outer(jnp.concatenate(both + [last], axis=1))

    lower = iota((16, 128), 1) < BLOCK

    def turned(value):
        return pltpu.roll(value, BLOCK, 1)

    def move_sems(m, first):
        return move_send_sem.at[m, first // 4], move_recv_sem.at[m, first // 4]

    def moves(m, first):
        return all_of(got.at[m, 4:6] if first else got.at[m, 0:4], *move_sems(m, first))

    def send_moves(m, first, block):
        for t in range(block.shape[1] // 128):
            tile = block[:, 128 * t : 128 * (t + 1)]
            k = first + 2 * t
            packed[m, k] = jnp.where(lower, tile[:16], turned(tile[16:]))
            packed[m, k + 1] = jnp.where(lower, turned(tile[:16]), tile[16:])
            for i in (k, k + 1):
                remote_copy(
                    packed.at[m, i], got.at[m, i], *move_sems(m, first), MOVE_STEPS[i]
                ).start()

    def arrivals(m, first):
        moves(m, first).wait_recv()
        tiles = []
        for k in (4,) if first else (0, 2):
            one, two = got[m, k], got[m, k + 1]
            top = jnp.where(lower, one, turned(two))
            bottom = jnp.where(lower, turned(one), two)
            tiles.append(jnp.concatenate([top, bottom], axis=0))
        return jnp.concatenate(tiles, axis=1)

    def sent(h):
        for kind in range(3):
            halo_kind(h, kind).wait_send()

    plane[0] = jnp.zeros((2, PLANE, 128), F32)
    x_send[...] = jnp.zeros(x_send.shape, F32)
    same_z = jnp.where(iota((PLANE, SIDE), 0) & 7 == iota((PLANE, SIDE), 1), 1.0, 0.0)
    same_y = iota((PLANE, PLANE), 0) >> 3 == iota((PLANE, PLANE), 1) & 7
    goes = (iota((PLANE, SIDE * LANES), 0) >> 3) * LANES + 20
    goes = jnp.where(iota((PLANE, SIDE * LANES), 1) == goes, 1.0, 0.0).astype(BF16)
    rate = jnp.zeros((PLANE, SIDE * LANES), F32)
    for part in parts(load("mix_rate")[...]):
        along_z = jnp.where(same_y, dot_nt(same_z.astype(BF16), part), 0.0)
        rate = rate + dot(along_z.astype(BF16), goes)
    mean_ref = load("mean_field")
    for x in range(SIDE):
        base = LANES * (x % 4)
        plane[0, x // 4, :, base : base + 20] = mean_ref[PLANE * x : PLANE * (x + 1), :]
    inner1 = jnp.concatenate([plane[0, 0], plane[0, 1]], axis=1) + rate
    put(0, inner1)
    prepare_corners(0)
    prepare_z(0)
    field1 = compact(inner1.T)
    prepare_x(0, field1)

    pl.semaphore_wait(barrier, len(halo_steps))
    send_y(0)
    send_z(0)
    send_x(0)

    ok = [
        jnp.where(gx > 0, 1.0, 0.0),
        jnp.where(gx < n_gx - 1, 1.0, 0.0),
        jnp.where(gy > 0, 1.0, 0.0),
        jnp.where(gy < n_gy - 1, 1.0, 0.0),
    ]

    cell1 = load("cell_first")
    off1 = load("offset_first")
    face1 = load("face_first")
    cell2 = load("cell_second")
    cell3 = load("cell_final")
    mass = load("particle_mass")
    off2 = load("offset_second")
    pay[0:20, :] = load("scalars")[...]
    pay[20:21, :] = mass[...]
    pay[21:24, :] = off2[...]
    pay[24:25, :] = cell2[...].astype(F32)
    pay[25:26, :] = cell3[...].astype(F32)
    pay[26:27, :] = cell1[...].astype(F32)
    pay[27:30, :] = off1[...]
    pay[30:32, :] = jnp.zeros((2, pay.shape[1]), F32)

    def packed_movers(faces):
        slots = slots_of(faces)
        hot = [slots_hot(slots[:, lanes]) for lanes in OWN]
        left = [pack_operand(pay[:, lanes]) for lanes in OWN]
        block = sum(dot_nt(a, b) for a, b in zip(left, hot))
        return block[:32] + block[32:]

    def weights_at(cells, offsets, lanes):
        return weights(cells[:, lanes], [offsets[d : d + 1, lanes] for d in range(3)], ok)

    def scalars_of(block):
        row = iota((ROWS, block.shape[1]), 0)
        return jnp.where(row == 20, 1.0, jnp.where(row < 20, block[:ROWS], 0.0))

    def message(values, block):
        row = iota((ROWS, block.shape[1]), 0)
        return jnp.concatenate([jnp.where(row < 20, values, block[:ROWS]), block[ROWS:]], axis=0)

    def work(values, sampled, outer, ws):
        more = gather(outer, ws, 1)
        return react(values, [a + b for a, b in zip(sampled, more)], first, second)

    def work_movers(m, movers, inner, outer, ws):
        blocks = [movers[:, lanes] for lanes in (FAR, NEAR)]
        new = work([scalars_of(block) for block in blocks], inner, outer, ws)
        messages = [message(one, block) for one, block in zip(new, blocks)]
        for first, one in zip((4, 0), messages):
            send_moves(m, first, one)

    movers = packed_movers(face1[...])
    mover_cells = movers[26:27].astype(jnp.int32)
    w_movers = [weights_at(mover_cells, movers[27:30], lanes) for lanes in (FAR, NEAR)]

    rows_buf[...] = jnp.zeros(rows_buf.shape, F32)
    rows_buf[0, 0:20, :] = load("react_in")[...]
    rows_buf[0, 20:21, :] = load("hidden_bias")[...]
    rows_buf[1, 0:20, :] = load("react_out")[...]
    high, low = parts_wide(rows_buf[0])
    first = jnp.concatenate(
        [high, high, low, jnp.zeros((128 - 3 * ROWS, 128), F32)], axis=0
    ).T.astype(BF16)
    high, low = parts_wide(rows_buf[1])
    second = jnp.concatenate(
        [
            jnp.concatenate([high, high], axis=1),
            jnp.concatenate([low, jnp.zeros_like(low)], axis=1),
        ],
        axis=0,
    ).astype(BF16)

    left = inner_left(0, field1)
    in_movers = gather(left, w_movers, 0)
    w_own = [weights_at(cell1, off1, lanes) for lanes in OWN]
    in_own = gather(left, w_own, 0)

    outer = outer_left(0)
    work_movers(0, movers, in_movers, outer, w_movers)

    values = work([scalars_of(pay[:, lanes]) for lanes in OWN], in_own, outer, w_own)
    stay = [jnp.where(face1[:, lanes] == 0, mass[:, lanes], 0.0) for lanes in OWN]
    sums = scatter([(v, m, cell2[:, lanes]) for v, m, lanes in zip(values, stay, OWN)])
    for one, lanes in zip(values, OWN):
        pay[0:20, lanes] = one[:20]

    lane = iota((1, 128), 1)
    alive = {
        0: jnp.concatenate([jnp.where(lane < 64, ok[0], ok[1]), jnp.ones((1, 128), F32)], axis=1),
        4: jnp.where(lane < 64, ok[2], ok[3]),
    }

    came = {}
    for i in (0, 4):
        block = arrivals(0, i)
        came[i] = block
        cells = block[24:25].astype(jnp.int32)
        sums = sums + scatter([(scalars_of(block), block[20:21] * alive[i], cells)])
    field2 = average(by_cell(sums), field1)
    put(1, spread(field2).T)
    prepare_corners(1)
    send_y(1)
    prepare_z(1)
    send_z(1)
    prepare_x(1, field2)
    send_x(1)

    face2 = load("face_second")
    movers = packed_movers(face2[...])
    mover_cells = movers[24:25].astype(jnp.int32)
    w_movers = [weights_at(mover_cells, movers[21:24], lanes) for lanes in (FAR, NEAR)]
    left = inner_left(1, field2)
    in_movers = gather(left, w_movers, 0)
    w_own = [weights_at(cell2, off2, lanes) for lanes in OWN]
    w_own += [
        weights_at(block[24:25].astype(jnp.int32), block[21:24], slice(None))
        for block in came.values()
    ]
    in_own = gather(left, w_own, 0)

    outer = outer_left(1)
    work_movers(1, movers, in_movers, outer, w_movers)

    values = work(values + [scalars_of(block) for block in came.values()], in_own, outer, w_own)
    masses = [
        jnp.where(face1[:, lanes] + face2[:, lanes] == 0, mass[:, lanes], 0.0) for lanes in OWN
    ] + [block[20:21] * alive[i] for i, block in came.items()]
    cells = [cell3[:, lanes] for lanes in OWN]
    cells += [block[25:26].astype(jnp.int32) for block in came.values()]
    sums = scatter(list(zip(values, masses, cells)))

    sent(0)
    sent(1)
    for i in (0, 4):
        moves(0, i).wait_send()

    for i in (0, 4):
        block = arrivals(1, i)
        cells = block[25:26].astype(jnp.int32)
        sums = sums + scatter([(scalars_of(block), block[20:21] * alive[i], cells)])
    sums = by_cell(sums)
    result = spread(average(sums, field2)).T
    for x in range(SIDE):
        out_ref[PLANE * x : PLANE * (x + 1), :] = result[:, LANES * x : LANES * x + 20]

    for i in (0, 4):
        moves(1, i).wait_send()


def shards(
    sizes,
    scalars,
    particle_mass,
    cell_first,
    cell_second,
    cell_final,
    offset_first,
    offset_second,
    face_first,
    face_second,
    mean_field,
    mix_rate,
    react_in,
    hidden_bias,
    react_out,
):
    row = lambda a: a.reshape(1, -1)
    operands = [
        scalars,
        row(particle_mass),
        row(cell_first),
        row(cell_second),
        row(cell_final),
        offset_first,
        offset_second,
        row(face_first),
        row(face_second),
        mean_field.transpose(1, 2, 3, 0).reshape(SIDE * PLANE, 20),
        mix_rate.reshape(PLANE, SIDE),
        react_in.T,
        row(hidden_bias),
        react_out,
    ]
    operands = [pltpu.with_memory_space_constraint(a, pltpu.HBM) for a in operands]
    vmem = pl.BlockSpec(memory_space=pltpu.VMEM)
    result = pl.pallas_call(
        functools.partial(kernel, sizes),
        out_shape=jax.ShapeDtypeStruct((SIDE * PLANE, 20), F32),
        in_specs=[pl.BlockSpec(memory_space=pltpu.HBM)] * len(operands),
        out_specs=vmem,
        scratch_shapes=[pltpu.VMEM(a.shape, a.dtype) for a in operands]
        + [
            pltpu.VMEM((2, 2, PLANE, 128), F32),
            pltpu.VMEM((2, 2, 2, SIDE, 128), F32),
            pltpu.VMEM((2, 4, 2, 1, 128), F32),
            pltpu.VMEM((2, 2, ROWS, 128), F32),
            pltpu.VMEM((2, 16, SIDE, 128), F32),
            pltpu.VMEM((2, 16, 1, 128), F32),
            pltpu.VMEM((2, 2, ROWS, 128), F32),
            pltpu.VMEM((2, 6, 16, 128), F32),
            pltpu.VMEM((2, 6, 16, 128), F32),
            pltpu.VMEM((2, ROWS, 128), F32),
            pltpu.VMEM((32, 1024), F32),
            pltpu.SemaphoreType.DMA((INPUTS,)),
            pltpu.SemaphoreType.DMA((2, 3)),
            pltpu.SemaphoreType.DMA((2, 3)),
            pltpu.SemaphoreType.DMA((2, 2)),
            pltpu.SemaphoreType.DMA((2, 2)),
        ],
        compiler_params=pltpu.CompilerParams(
            collective_id=0, has_side_effects=True, vmem_limit_bytes=40 * 1024 * 1024
        ),
    )(*operands)
    return result.reshape(SIDE, SIDE, SIDE, 20).transpose(3, 0, 1, 2)


def solution(mesh):
    particles = P(("gx", "gy", "gz"))
    in_specs = (
        P(None, ("gx", "gy", "gz")),
        particles,
        particles,
        particles,
        particles,
        P(None, ("gx", "gy", "gz")),
        P(None, ("gx", "gy", "gz")),
        particles,
        particles,
        P(None, "gx", "gy", "gz"),
        P("gx", "gy", "gz"),
        P(),
        P(),
        P(),
    )
    sizes = (mesh.shape["gx"], mesh.shape["gy"], mesh.shape["gz"])
    return jax.shard_map(
        functools.partial(shards, sizes),
        mesh=mesh,
        in_specs=in_specs,
        out_specs=P(None, "gx", "gy", "gz"),
        check_vma=False,
    )
```

```python
import functools

import jax
import jax.numpy as jnp
from jax import lax
from jax.experimental import pallas as pl
from jax.experimental.pallas import tpu as pltpu
from jax.sharding import PartitionSpec as P

MESH = pl.DeviceIdType.MESH
F32 = jnp.float32
BF16 = jnp.bfloat16

IEM_FACTOR = 0.4
TIME_STEP = 0.4
PRIOR_MASS = 2.0

ROWS = 24
LANES = 32
SIDE = 8
PLANE = 64
BLOCK = 64

NAMES = [
    "scalars",
    "particle_mass",
    "cell_first",
    "cell_second",
    "cell_final",
    "offset_first",
    "offset_second",
    "face_first",
    "face_second",
    "mean_field",
    "mix_rate",
    "react_in",
    "hidden_bias",
    "react_out",
]
INPUTS = len(NAMES)
ORDER = ["mean_field", "mix_rate", "cell_first", "offset_first", "react_in", "hidden_bias"]
ORDER += ["react_out", "face_first", "face_second", "cell_second", "cell_final"]
ORDER += ["particle_mass", "offset_second", "scalars"]

MOVE_STEPS = [(1, 0, 0), (-1, 0, 0), (0, 0, 1), (0, 0, -1), (0, 1, 0), (0, -1, 0)]

OWN = [slice(i, i + 256) for i in range(0, 1024, 256)]
NEAR, FAR = slice(0, 256), slice(256, 384)

NT = (((1,), (1,)), ((), ()))


def dot(a, b):
    return jnp.dot(a, b, preferred_element_type=F32)


def dot_nt(a, b):
    return lax.dot_general(a, b, NT, preferred_element_type=F32)


def parts(v):
    high = v.astype(BF16)
    return high, (v - high.astype(F32)).astype(BF16)


def parts_wide(v):
    high = v.astype(BF16).astype(F32)
    return high, v - high


def iota(shape, dim):
    return lax.broadcasted_iota(jnp.int32, shape, dim)


def spline(u):
    return 0.5 * (0.5 - u) ** 2, 0.75 - u * u, 0.5 * (0.5 + u) ** 2


def along(cell, offset, low_ok, high_ok):
    low, mid, high = spline(offset)
    away = iota((SIDE, cell.shape[1]), 0) - cell
    inner = jnp.where(
        away == 0, mid, jnp.where(away == 1, high, jnp.where(away == -1, low, 0.0))
    )
    return (
        inner,
        jnp.where(cell == 0, low, 0.0) * low_ok,
        jnp.where(cell == SIDE - 1, high, 0.0) * high_ok,
    )


def weights(cells, offsets, ok):
    x_in, x_low, x_high = along(cells >> 6, offsets[0], ok[0], ok[1])
    y_in, y_low, y_high = along((cells >> 3) & 7, offsets[1], ok[2], ok[3])
    z_in, z_low, z_high = along(cells & 7, offsets[2], 1.0, 1.0)
    inner = jnp.concatenate([z_in * y_in[y : y + 1] for y in range(SIDE)], axis=0)
    row = iota(z_in.shape, 0)
    corner = jnp.where(
        row == 0,
        y_low * z_low,
        jnp.where(
            row == 1,
            y_low * z_high,
            jnp.where(row == 2, y_high * z_low, jnp.where(row == 3, y_high * z_high, 0.0)),
        ),
    )
    outer = jnp.concatenate(
        [z_in * y_low, z_in * y_high, y_in * z_low, y_in * z_high, corner, jnp.zeros_like(corner)],
        axis=0,
    )
    none = jnp.zeros((PLANE - outer.shape[0], cells.shape[1]), BF16)
    high, low = parts(outer)
    outer = jnp.concatenate([high, none, high, none, low, none], axis=0)
    return three_parts(*parts(inner)), outer, x_in, x_low, x_high


def compact(field):
    return jnp.concatenate([field[LANES * x : LANES * x + ROWS] for x in range(SIDE)], axis=0)


def spread(field):
    none = jnp.zeros((LANES - ROWS, field.shape[1]), field.dtype)
    pieces = []
    for x in range(SIDE):
        pieces += [field[ROWS * x : ROWS * (x + 1)], none]
    return jnp.concatenate(pieces, axis=0)


def three_parts(high, low):
    return jnp.concatenate([high, high, low], axis=0)


def left_of(field):
    high, low = parts_wide(field)
    return jnp.concatenate([high, low, high], axis=1).astype(BF16)


def left_outer(outer):
    high, low = parts_wide(outer)
    turned = jnp.concatenate([high, low], axis=0).T
    base = SIDE * LANES
    rows = jnp.concatenate(
        [
            compact(turned[:base]),
            turned[base + 3 * LANES : base + 3 * LANES + ROWS],
            turned[base : base + ROWS],
        ],
        axis=0,
    )
    return jnp.concatenate([rows, rows[:, :PLANE]], axis=1).astype(BF16)


def gather_own(result, x_in):
    total = x_in[0:1] * result[:ROWS]
    for x in range(1, SIDE):
        total = total + x_in[x : x + 1] * result[ROWS * x : ROWS * (x + 1)]
    return total


def gather(left, ws, which):
    results = [dot(left, w[which]) for w in ws]
    totals = []
    for result, w in zip(results, ws):
        sides = result[SIDE * ROWS :]
        own = gather_own(result, w[2])
        totals.append(own + w[3] * sides[:ROWS] + w[4] * sides[ROWS:])
    return totals


def mix(values, sampled):
    mixed = values - IEM_FACTOR * sampled[20:21] * (values - sampled)
    return jnp.where(iota(mixed.shape, 0) == 20, 1.0, mixed)


def first_operand(mixed):
    high, low = parts_wide(mixed)
    none = jnp.zeros((128 - 3 * ROWS, mixed.shape[1]), F32)
    return jnp.concatenate([high, low, high, none], axis=0).astype(BF16)


def react(values, sampled, first, second):
    mixed = [mix(one, sample) for one, sample in zip(values, sampled)]
    operands = [first_operand(one) for one in mixed]
    hidden = [dot(first, one) for one in operands]
    hidden = [jnp.concatenate(parts(jnp.tanh(one)), axis=0) for one in hidden]
    results = [dot(second, one) for one in hidden]
    return [one + TIME_STEP * (result[:ROWS] + result[ROWS:]) for one, result in zip(mixed, results)]


def slots_of(faces):
    count = faces.shape[1]
    code = iota((SIDE, count), 0)
    own_code = jnp.where(code < 2, code + 1, jnp.where(code < 4, code + 3, code - 1))
    chosen = (own_code == faces) & (code < 6)
    mask = jnp.where(chosen, 1.0, 0.0)
    chunks = count // 128
    stacked = jnp.concatenate(
        [mask[:, 128 * j : 128 * (j + 1)] for j in range(chunks)], axis=0
    ).astype(BF16)
    row, col = iota((128, 256), 0), iota((128, 256), 1)
    counter = jnp.where((row < col) | (col >= 128), 1.0, 0.0).astype(BF16)
    ranks = dot(stacked, counter)
    before = jnp.zeros((SIDE, 128), F32)
    pieces = []
    for j in range(chunks):
        rows = slice(SIDE * j, SIDE * (j + 1))
        pieces.append(ranks[rows, :128] + before)
        before = before + ranks[rows, 128:]
    rank = jnp.concatenate(pieces, axis=1)
    place = jnp.where(chosen, rank.astype(jnp.int32) + BLOCK * code + 1, 0)
    return jnp.sum(place, axis=0, keepdims=True) - 1


def one_hot(index, size):
    shape = (16, index.shape[1])
    away = iota(shape, 0).astype(F32).astype(BF16)
    away = away - jnp.broadcast_to(index.astype(F32), shape).astype(BF16)
    one, zero = jnp.ones(shape, BF16), jnp.zeros(shape, BF16)
    return jnp.concatenate(
        [jnp.where(away == jnp.full(shape, -16.0 * b, BF16), one, zero) for b in range(size // 16)],
        axis=0,
    )


def pack_operand(payload):
    return jnp.concatenate(parts_wide(payload), axis=0).astype(BF16)


def slots_hot(slots):
    return jnp.concatenate([one_hot(slots, 256), one_hot(slots - 256, 128)], axis=0)


def scatter_operand(values, masses, cells):
    high, low = parts_wide(values * masses)
    stacked = jnp.concatenate([high, low], axis=0)
    upper = (cells >> 8).astype(F32)
    return jnp.concatenate([stacked * (1.0 - upper), stacked * upper], axis=0).astype(BF16)


def scatter(group):
    hot = [one_hot(cells & 255, 4 * PLANE) for _, _, cells in group]
    left = [scatter_operand(*one) for one in group]
    return sum(dot_nt(a, b) for a, b in zip(left, hot))


def by_cell(result):
    pieces = []
    for x in range(SIDE):
        base = 2 * ROWS * (x // 4)
        lanes = slice(PLANE * (x % 4), PLANE * (x % 4 + 1))
        pieces.append(result[base : base + ROWS, lanes] + result[base + ROWS : base + 2 * ROWS, lanes])
    return jnp.concatenate(pieces, axis=0)


def average(sums, field):
    pieces = []
    for x in range(SIDE):
        rows = slice(ROWS * x, ROWS * (x + 1))
        one, old = sums[rows], field[rows]
        new = (one + PRIOR_MASS * old) / (one[20:21] + PRIOR_MASS)
        pieces.append(jnp.where(iota(new.shape, 0) == 20, old, new))
    return jnp.concatenate(pieces, axis=0)


def kernel(sizes, *refs):
    inputs, out_ref, refs = refs[:INPUTS], refs[INPUTS], refs[INPUTS + 1 :]
    local, refs = refs[:INPUTS], refs[INPUTS:]
    (
        plane,
        z_send,
        c_send,
        x_send,
        tile_got,
        row_got,
        x_got,
        packed,
        got,
        rows_buf,
        pay,
        local_sem,
        halo_send_sem,
        halo_recv_sem,
        move_send_sem,
        move_recv_sem,
    ) = refs
    n_gx, n_gy, n_gz = sizes
    gx, gy, gz = lax.axis_index("gx"), lax.axis_index("gy"), lax.axis_index("gz")

    def three(index, size):
        return {-1: lax.rem(index + size - 1, size), 0: index, 1: lax.rem(index + 1, size)}

    near_x, near_y, near_z = three(gx, n_gx), three(gy, n_gy), three(gz, n_gz)

    def at(dx, dy, dz):
        return near_x[dx], near_y[dy], near_z[dz]

    faces = [(1, 0), (-1, 0), (0, 1), (0, -1)]
    corners = [(1, 1), (1, -1), (-1, 1), (-1, -1)]
    x_steps = [1, -1]
    halo_steps = [(dx, dy, dz) for dx in x_steps for dy, dz in corners]
    halo_steps += [(0, dy, dz) for dy, dz in corners]
    halo_steps += [(dx, dy, 0) for dx in x_steps for dy in (1, -1)]
    halo_steps += [(0, dy, 0) for dy in (1, -1)]
    halo_steps += [(dx, 0, dz) for dx in x_steps for dz in (1, -1)]
    halo_steps += [(0, 0, dz) for dz in (1, -1)]
    halo_steps += [(dx, 0, 0) for dx in x_steps]

    loads = {
        name: pltpu.make_async_copy(a, to, local_sem.at[i])
        for i, (name, a, to) in enumerate(zip(NAMES, inputs, local))
    }
    barrier = pltpu.get_barrier_semaphore()
    for step in halo_steps:
        pl.semaphore_signal(barrier, inc=1, device_id=at(*step), device_id_type=MESH)
    for name in ORDER:
        loads[name].start()

    def load(name):
        loads[name].wait()
        return local[NAMES.index(name)]

    def remote_copy(src, dst, send_sem, recv_sem, step):
        return pltpu.make_async_remote_copy(
            src_ref=src,
            dst_ref=dst,
            send_sem=send_sem,
            recv_sem=recv_sem,
            device_id=at(*step),
            device_id_type=MESH,
        )

    def put(h, value):
        plane[h, 0] = value[:, :128]
        plane[h, 1] = value[:, 128:]

    def all_of(buffer, send_sem, recv_sem):
        return remote_copy(buffer, buffer, send_sem, recv_sem, (1, 0, 0))

    def halo_kind(h, kind):
        buffer = (tile_got, row_got, x_got)[kind].at[h]
        return all_of(buffer, halo_send_sem.at[h, kind], halo_recv_sem.at[h, kind])

    def send_halo(h, first, kind, source, target):
        for i, (src, dst) in enumerate(zip(source, target)):
            remote_copy(
                src, dst, halo_send_sem.at[h, kind], halo_recv_sem.at[h, kind], halo_steps[first + i]
            ).start()

    def prepare_x(h, field):
        x_send[h, 0, :, 0:PLANE] = field[7 * ROWS : 8 * ROWS]
        x_send[h, 1, :, 0:PLANE] = field[0:ROWS]

    def send_x(h):
        send_halo(h, 24, 2, [x_send.at[h, k] for k in range(2)], [x_got.at[h, k] for k in range(2)])

    def prepare_corners(h):
        for slot, row in enumerate((63, 56, 7, 0)):
            for half in range(2):
                c_send[h, slot, half] = plane[h, half, row : row + 1, :]

    def prepare_z(h):
        for z, slot in ((7, 0), (0, 1)):
            for half in range(2):
                z_send[h, slot, half] = plane[h, half, pl.ds(z, SIDE, stride=SIDE), :]

    def send_y(h):
        sides = ((0, 1), (1, 0))
        source = [c_send.at[h, slot, half] for _, half in sides for slot in range(4)]
        target = [row_got.at[h, 8 + 4 * k + slot] for k, _ in sides for slot in range(4)]
        source += [c_send.at[h, slot] for slot in range(4)]
        target += [row_got.at[h, 2 * slot : 2 * slot + 2] for slot in range(4)]
        send_halo(h, 0, 1, source, target)
        rows = plane.at[h]
        y_rows = (slice(56, 64), slice(0, 8))
        source = [rows.at[half, y] for _, half in sides for y in y_rows]
        target = [tile_got.at[h, 8 + 4 * k + slot] for k, _ in sides for slot in range(2)]
        source += [rows.at[:, y] for y in y_rows]
        target += [tile_got.at[h, 2 * slot : 2 * slot + 2] for slot in range(2)]
        send_halo(h, 12, 0, source, target)

    def send_z(h):
        sides = ((0, 1), (1, 0))
        source = [z_send.at[h, slot, half] for _, half in sides for slot in range(2)]
        target = [tile_got.at[h, 10 + 4 * k + slot] for k, _ in sides for slot in range(2)]
        source += [z_send.at[h, slot] for slot in range(2)]
        target += [tile_got.at[h, 4 + 2 * slot : 6 + 2 * slot] for slot in range(2)]
        send_halo(h, 18, 0, source, target)

    def stack_outer(face, corner):
        row = iota((SIDE, 128), 0)
        last = jnp.zeros((SIDE, 128), F32)
        for slot in range(4):
            last = jnp.where(row == slot, corner[slot], last)
        none = jnp.zeros((PLANE - 5 * SIDE, 128), F32)
        return jnp.concatenate(face + [last, none], axis=0)

    def inner_left(h, field):
        halo_kind(h, 2).wait_recv()
        sides = jnp.concatenate([x_got[h, 0], x_got[h, 1]], axis=0)[:, :PLANE]
        return jnp.concatenate([left_of(field), left_of(sides)], axis=0)

    def outer_left(h):
        for kind in range(2):
            halo_kind(h, kind).wait_recv()
        both = [
            stack_outer(
                [tile_got[h, 2 * slot + half] for slot in range(4)],
                [row_got[h, 2 * slot + half] for slot in range(4)],
            )
            for half in range(2)
        ]
        side = [
            stack_outer(
                [tile_got[h, 8 + 4 * k + slot] for slot in range(4)],
                [row_got[h, 8 + 4 * k + slot] for slot in range(4)],
            )
            for k in range(2)
        ]
        last = jnp.where(iota((PLANE, 128), 1) < PLANE, side[1], side[0])
        return left_outer(jnp.concatenate(both + [last], axis=1))

    lower = iota((16, 128), 1) < BLOCK

    def turned(value):
        return pltpu.roll(value, BLOCK, 1)

    def move_sems(m, first):
        return move_send_sem.at[m, first // 4], move_recv_sem.at[m, first // 4]

    def moves(m, first):
        return all_of(got.at[m, 4:6] if first else got.at[m, 0:4], *move_sems(m, first))

    def send_moves(m, first, block):
        for t in range(block.shape[1] // 128):
            tile = block[:, 128 * t : 128 * (t + 1)]
            k = first + 2 * t
            packed[m, k] = jnp.where(lower, tile[:16], turned(tile[16:]))
            packed[m, k + 1] = jnp.where(lower, turned(tile[:16]), tile[16:])
            for i in (k, k + 1):
                remote_copy(
                    packed.at[m, i], got.at[m, i], *move_sems(m, first), MOVE_STEPS[i]
                ).start()

    def arrivals(m, first):
        moves(m, first).wait_recv()
        tiles = []
        for k in (4,) if first else (0, 2):
            one, two = got[m, k], got[m, k + 1]
            top = jnp.where(lower, one, turned(two))
            bottom = jnp.where(lower, turned(one), two)
            tiles.append(jnp.concatenate([top, bottom], axis=0))
        return jnp.concatenate(tiles, axis=1)

    def sent(h):
        for kind in range(3):
            halo_kind(h, kind).wait_send()

    plane[0] = jnp.zeros((2, PLANE, 128), F32)
    x_send[...] = jnp.zeros(x_send.shape, F32)
    same_z = jnp.where(iota((PLANE, SIDE), 0) & 7 == iota((PLANE, SIDE), 1), 1.0, 0.0)
    same_y = iota((PLANE, PLANE), 0) >> 3 == iota((PLANE, PLANE), 1) & 7
    goes = (iota((PLANE, SIDE * LANES), 0) >> 3) * LANES + 20
    goes = jnp.where(iota((PLANE, SIDE * LANES), 1) == goes, 1.0, 0.0).astype(BF16)
    rate = jnp.zeros((PLANE, SIDE * LANES), F32)
    for part in parts(load("mix_rate")[...]):
        along_z = jnp.where(same_y, dot_nt(same_z.astype(BF16), part), 0.0)
        rate = rate + dot(along_z.astype(BF16), goes)
    mean_ref = load("mean_field")
    for x in range(SIDE):
        base = LANES * (x % 4)
        plane[0, x // 4, :, base : base + 20] = mean_ref[PLANE * x : PLANE * (x + 1), :]
    inner1 = jnp.concatenate([plane[0, 0], plane[0, 1]], axis=1) + rate
    put(0, inner1)
    prepare_corners(0)
    prepare_z(0)
    field1 = compact(inner1.T)
    prepare_x(0, field1)

    pl.semaphore_wait(barrier, len(halo_steps))
    send_y(0)
    send_x(0)
    send_z(0)

    ok = [
        jnp.where(gx > 0, 1.0, 0.0),
        jnp.where(gx < n_gx - 1, 1.0, 0.0),
        jnp.where(gy > 0, 1.0, 0.0),
        jnp.where(gy < n_gy - 1, 1.0, 0.0),
    ]

    cell1 = load("cell_first")
    off1 = load("offset_first")
    face1 = load("face_first")
    cell2 = load("cell_second")
    cell3 = load("cell_final")
    mass = load("particle_mass")
    off2 = load("offset_second")
    pay[0:20, :] = load("scalars")[...]
    pay[20:21, :] = mass[...]
    pay[21:24, :] = off2[...]
    pay[24:25, :] = cell2[...].astype(F32)
    pay[25:26, :] = cell3[...].astype(F32)
    pay[26:27, :] = cell1[...].astype(F32)
    pay[27:30, :] = off1[...]
    pay[30:32, :] = jnp.zeros((2, pay.shape[1]), F32)

    def packed_movers(faces):
        slots = slots_of(faces)
        hot = [slots_hot(slots[:, lanes]) for lanes in OWN]
        left = [pack_operand(pay[:, lanes]) for lanes in OWN]
        block = sum(dot_nt(a, b) for a, b in zip(left, hot))
        return block[:32] + block[32:]

    def weights_at(cells, offsets, lanes):
        return weights(cells[:, lanes], [offsets[d : d + 1, lanes] for d in range(3)], ok)

    def scalars_of(block):
        row = iota((ROWS, block.shape[1]), 0)
        return jnp.where(row == 20, 1.0, jnp.where(row < 20, block[:ROWS], 0.0))

    def message(values, block):
        row = iota((ROWS, block.shape[1]), 0)
        return jnp.concatenate([jnp.where(row < 20, values, block[:ROWS]), block[ROWS:]], axis=0)

    def work(values, sampled, outer, ws):
        more = gather(outer, ws, 1)
        return react(values, [a + b for a, b in zip(sampled, more)], first, second)

    def work_movers(m, movers, inner, outer, ws):
        blocks = [movers[:, lanes] for lanes in (FAR, NEAR)]
        new = work([scalars_of(block) for block in blocks], inner, outer, ws)
        messages = [message(one, block) for one, block in zip(new, blocks)]
        for first, one in zip((4, 0), messages):
            send_moves(m, first, one)

    movers = packed_movers(face1[...])
    mover_cells = movers[26:27].astype(jnp.int32)
    w_movers = [weights_at(mover_cells, movers[27:30], lanes) for lanes in (FAR, NEAR)]

    rows_buf[...] = jnp.zeros(rows_buf.shape, F32)
    rows_buf[0, 0:20, :] = load("react_in")[...]
    rows_buf[0, 20:21, :] = load("hidden_bias")[...]
    rows_buf[1, 0:20, :] = load("react_out")[...]
    high, low = parts_wide(rows_buf[0])
    first = jnp.concatenate(
        [high, high, low, jnp.zeros((128 - 3 * ROWS, 128), F32)], axis=0
    ).T.astype(BF16)
    high, low = parts_wide(rows_buf[1])
    second = jnp.concatenate(
        [
            jnp.concatenate([high, high], axis=1),
            jnp.concatenate([low, jnp.zeros_like(low)], axis=1),
        ],
        axis=0,
    ).astype(BF16)

    w_own = [weights_at(cell1, off1, lanes) for lanes in OWN]
    left = inner_left(0, field1)
    in_movers = gather(left, w_movers, 0)
    in_own = gather(left, w_own, 0)

    outer = outer_left(0)
    work_movers(0, movers, in_movers, outer, w_movers)

    values = work([scalars_of(pay[:, lanes]) for lanes in OWN], in_own, outer, w_own)
    stay = [jnp.where(face1[:, lanes] == 0, mass[:, lanes], 0.0) for lanes in OWN]
    sums = scatter([(v, m, cell2[:, lanes]) for v, m, lanes in zip(values, stay, OWN)])
    for one, lanes in zip(values, OWN):
        pay[0:20, lanes] = one[:20]

    lane = iota((1, 128), 1)
    alive = {
        0: jnp.concatenate([jnp.where(lane < 64, ok[0], ok[1]), jnp.ones((1, 128), F32)], axis=1),
        4: jnp.where(lane < 64, ok[2], ok[3]),
    }

    came = {}
    for i in (0, 4):
        block = arrivals(0, i)
        came[i] = block
        cells = block[24:25].astype(jnp.int32)
        sums = sums + scatter([(scalars_of(block), block[20:21] * alive[i], cells)])
    field2 = average(by_cell(sums), field1)
    put(1, spread(field2).T)
    prepare_corners(1)
    send_y(1)
    prepare_x(1, field2)
    send_x(1)
    prepare_z(1)
    send_z(1)

    face2 = load("face_second")
    movers = packed_movers(face2[...])
    mover_cells = movers[24:25].astype(jnp.int32)
    w_movers = [weights_at(mover_cells, movers[21:24], lanes) for lanes in (FAR, NEAR)]
    w_own = [weights_at(cell2, off2, lanes) for lanes in OWN]
    w_own += [
        weights_at(block[24:25].astype(jnp.int32), block[21:24], slice(None))
        for block in came.values()
    ]
    left = inner_left(1, field2)
    in_movers = gather(left, w_movers, 0)
    in_own = gather(left, w_own, 0)

    outer = outer_left(1)
    work_movers(1, movers, in_movers, outer, w_movers)

    values = work(values + [scalars_of(block) for block in came.values()], in_own, outer, w_own)
    masses = [
        jnp.where(face1[:, lanes] + face2[:, lanes] == 0, mass[:, lanes], 0.0) for lanes in OWN
    ] + [block[20:21] * alive[i] for i, block in came.items()]
    cells = [cell3[:, lanes] for lanes in OWN]
    cells += [block[25:26].astype(jnp.int32) for block in came.values()]
    sums = scatter(list(zip(values, masses, cells)))

    sent(0)
    sent(1)
    for i in (0, 4):
        moves(0, i).wait_send()

    for i in (0, 4):
        block = arrivals(1, i)
        cells = block[25:26].astype(jnp.int32)
        sums = sums + scatter([(scalars_of(block), block[20:21] * alive[i], cells)])
    sums = by_cell(sums)
    result = spread(average(sums, field2)).T
    for x in range(SIDE):
        out_ref[PLANE * x : PLANE * (x + 1), :] = result[:, LANES * x : LANES * x + 20]

    for i in (0, 4):
        moves(1, i).wait_send()


def shards(
    sizes,
    scalars,
    particle_mass,
    cell_first,
    cell_second,
    cell_final,
    offset_first,
    offset_second,
    face_first,
    face_second,
    mean_field,
    mix_rate,
    react_in,
    hidden_bias,
    react_out,
):
    row = lambda a: a.reshape(1, -1)
    operands = [
        scalars,
        row(particle_mass),
        row(cell_first),
        row(cell_second),
        row(cell_final),
        offset_first,
        offset_second,
        row(face_first),
        row(face_second),
        mean_field.transpose(1, 2, 3, 0).reshape(SIDE * PLANE, 20),
        mix_rate.reshape(PLANE, SIDE),
        react_in.T,
        row(hidden_bias),
        react_out,
    ]
    operands = [pltpu.with_memory_space_constraint(a, pltpu.HBM) for a in operands]
    vmem = pl.BlockSpec(memory_space=pltpu.VMEM)
    result = pl.pallas_call(
        functools.partial(kernel, sizes),
        out_shape=jax.ShapeDtypeStruct((SIDE * PLANE, 20), F32),
        in_specs=[pl.BlockSpec(memory_space=pltpu.HBM)] * len(operands),
        out_specs=vmem,
        scratch_shapes=[pltpu.VMEM(a.shape, a.dtype) for a in operands]
        + [
            pltpu.VMEM((2, 2, PLANE, 128), F32),
            pltpu.VMEM((2, 2, 2, SIDE, 128), F32),
            pltpu.VMEM((2, 4, 2, 1, 128), F32),
            pltpu.VMEM((2, 2, ROWS, 128), F32),
            pltpu.VMEM((2, 16, SIDE, 128), F32),
            pltpu.VMEM((2, 16, 1, 128), F32),
            pltpu.VMEM((2, 2, ROWS, 128), F32),
            pltpu.VMEM((2, 6, 16, 128), F32),
            pltpu.VMEM((2, 6, 16, 128), F32),
            pltpu.VMEM((2, ROWS, 128), F32),
            pltpu.VMEM((32, 1024), F32),
            pltpu.SemaphoreType.DMA((INPUTS,)),
            pltpu.SemaphoreType.DMA((2, 3)),
            pltpu.SemaphoreType.DMA((2, 3)),
            pltpu.SemaphoreType.DMA((2, 2)),
            pltpu.SemaphoreType.DMA((2, 2)),
        ],
        compiler_params=pltpu.CompilerParams(
            collective_id=0, has_side_effects=True, vmem_limit_bytes=40 * 1024 * 1024
        ),
    )(*operands)
    return result.reshape(SIDE, SIDE, SIDE, 20).transpose(3, 0, 1, 2)


def solution(mesh):
    particles = P(("gx", "gy", "gz"))
    in_specs = (
        P(None, ("gx", "gy", "gz")),
        particles,
        particles,
        particles,
        particles,
        P(None, ("gx", "gy", "gz")),
        P(None, ("gx", "gy", "gz")),
        particles,
        particles,
        P(None, "gx", "gy", "gz"),
        P("gx", "gy", "gz"),
        P(),
        P(),
        P(),
    )
    sizes = (mesh.shape["gx"], mesh.shape["gy"], mesh.shape["gz"])
    return jax.shard_map(
        functools.partial(shards, sizes),
        mesh=mesh,
        in_specs=in_specs,
        out_specs=P(None, "gx", "gy", "gz"),
        check_vma=False,
    )
```

```python
import functools

import jax
import jax.numpy as jnp
from jax import lax
from jax.experimental import pallas as pl
from jax.experimental.pallas import tpu as pltpu
from jax.sharding import PartitionSpec as P

MESH = pl.DeviceIdType.MESH
F32 = jnp.float32
BF16 = jnp.bfloat16

IEM_FACTOR = 0.4
TIME_STEP = 0.4
PRIOR_MASS = 2.0

ROWS = 24
LANES = 32
SIDE = 8
PLANE = 64
BLOCK = 64

NAMES = [
    "scalars",
    "particle_mass",
    "cell_first",
    "cell_second",
    "cell_final",
    "offset_first",
    "offset_second",
    "face_first",
    "face_second",
    "mean_field",
    "mix_rate",
    "react_in",
    "hidden_bias",
    "react_out",
]
INPUTS = len(NAMES)
ORDER = ["mean_field", "mix_rate", "cell_first", "offset_first", "react_in", "hidden_bias"]
ORDER += ["react_out", "face_first", "face_second", "cell_second", "cell_final"]
ORDER += ["particle_mass", "offset_second", "scalars"]

MOVE_STEPS = [(1, 0, 0), (-1, 0, 0), (0, 0, 1), (0, 0, -1), (0, 1, 0), (0, -1, 0)]

OWN = [slice(i, i + 256) for i in range(0, 1024, 256)]
NEAR, FAR = slice(0, 256), slice(256, 384)

NT = (((1,), (1,)), ((), ()))


def dot(a, b):
    return jnp.dot(a, b, preferred_element_type=F32)


def dot_nt(a, b):
    return lax.dot_general(a, b, NT, preferred_element_type=F32)


def parts(v):
    high = v.astype(BF16)
    return high, (v - high.astype(F32)).astype(BF16)


def parts_wide(v):
    high = v.astype(BF16).astype(F32)
    return high, v - high


def iota(shape, dim):
    return lax.broadcasted_iota(jnp.int32, shape, dim)


def spline(u):
    return 0.5 * (0.5 - u) ** 2, 0.75 - u * u, 0.5 * (0.5 + u) ** 2


def along(cell, offset, low_ok, high_ok):
    low, mid, high = spline(offset)
    away = iota((SIDE, cell.shape[1]), 0) - cell
    inner = jnp.where(
        away == 0, mid, jnp.where(away == 1, high, jnp.where(away == -1, low, 0.0))
    )
    return (
        inner,
        jnp.where(cell == 0, low, 0.0) * low_ok,
        jnp.where(cell == SIDE - 1, high, 0.0) * high_ok,
    )


def weights(cells, offsets, ok):
    x_in, x_low, x_high = along(cells >> 6, offsets[0], ok[0], ok[1])
    y_in, y_low, y_high = along((cells >> 3) & 7, offsets[1], ok[2], ok[3])
    z_in, z_low, z_high = along(cells & 7, offsets[2], 1.0, 1.0)
    inner = jnp.concatenate([z_in * y_in[y : y + 1] for y in range(SIDE)], axis=0)
    row = iota(z_in.shape, 0)
    corner = jnp.where(
        row == 0,
        y_low * z_low,
        jnp.where(
            row == 1,
            y_low * z_high,
            jnp.where(row == 2, y_high * z_low, jnp.where(row == 3, y_high * z_high, 0.0)),
        ),
    )
    outer = jnp.concatenate(
        [z_in * y_low, z_in * y_high, y_in * z_low, y_in * z_high, corner, jnp.zeros_like(corner)],
        axis=0,
    )
    none = jnp.zeros((PLANE - outer.shape[0], cells.shape[1]), BF16)
    high, low = parts(outer)
    outer = jnp.concatenate([high, none, high, none, low, none], axis=0)
    return three_parts(*parts(inner)), outer, x_in, x_low, x_high


def compact(field):
    return jnp.concatenate([field[LANES * x : LANES * x + ROWS] for x in range(SIDE)], axis=0)


def spread(field):
    none = jnp.zeros((LANES - ROWS, field.shape[1]), field.dtype)
    pieces = []
    for x in range(SIDE):
        pieces += [field[ROWS * x : ROWS * (x + 1)], none]
    return jnp.concatenate(pieces, axis=0)


def three_parts(high, low):
    return jnp.concatenate([high, high, low], axis=0)


def left_of(field):
    high, low = parts_wide(field)
    return jnp.concatenate([high, low, high], axis=1).astype(BF16)


def left_outer(outer):
    high, low = parts_wide(outer)
    turned = jnp.concatenate([high, low], axis=0).T
    base = SIDE * LANES
    rows = jnp.concatenate(
        [
            compact(turned[:base]),
            turned[base + 3 * LANES : base + 3 * LANES + ROWS],
            turned[base : base + ROWS],
        ],
        axis=0,
    )
    return jnp.concatenate([rows, rows[:, :PLANE]], axis=1).astype(BF16)


def gather_own(result, x_in):
    total = x_in[0:1] * result[:ROWS]
    for x in range(1, SIDE):
        total = total + x_in[x : x + 1] * result[ROWS * x : ROWS * (x + 1)]
    return total


def gather(left, ws, which):
    results = [dot(left, w[which]) for w in ws]
    totals = []
    for result, w in zip(results, ws):
        sides = result[SIDE * ROWS :]
        own = gather_own(result, w[2])
        totals.append(own + w[3] * sides[:ROWS] + w[4] * sides[ROWS:])
    return totals


def mix(values, sampled):
    mixed = values - IEM_FACTOR * sampled[20:21] * (values - sampled)
    return jnp.where(iota(mixed.shape, 0) == 20, 1.0, mixed)


def first_operand(mixed):
    high, low = parts_wide(mixed)
    none = jnp.zeros((128 - 3 * ROWS, mixed.shape[1]), F32)
    return jnp.concatenate([high, low, high, none], axis=0).astype(BF16)


def react(values, sampled, first, second):
    mixed = [mix(one, sample) for one, sample in zip(values, sampled)]
    operands = [first_operand(one) for one in mixed]
    hidden = [dot(first, one) for one in operands]
    hidden = [jnp.concatenate(parts(jnp.tanh(one)), axis=0) for one in hidden]
    results = [dot(second, one) for one in hidden]
    return [one + TIME_STEP * (result[:ROWS] + result[ROWS:]) for one, result in zip(mixed, results)]


def slots_of(faces):
    count = faces.shape[1]
    code = iota((SIDE, count), 0)
    own_code = jnp.where(code < 2, code + 1, jnp.where(code < 4, code + 3, code - 1))
    chosen = (own_code == faces) & (code < 6)
    mask = jnp.where(chosen, 1.0, 0.0)
    chunks = count // 128
    stacked = jnp.concatenate(
        [mask[:, 128 * j : 128 * (j + 1)] for j in range(chunks)], axis=0
    ).astype(BF16)
    row, col = iota((128, 256), 0), iota((128, 256), 1)
    counter = jnp.where((row < col) | (col >= 128), 1.0, 0.0).astype(BF16)
    ranks = dot(stacked, counter)
    before = jnp.zeros((SIDE, 128), F32)
    pieces = []
    for j in range(chunks):
        rows = slice(SIDE * j, SIDE * (j + 1))
        pieces.append(ranks[rows, :128] + before)
        before = before + ranks[rows, 128:]
    rank = jnp.concatenate(pieces, axis=1)
    place = jnp.where(chosen, rank.astype(jnp.int32) + BLOCK * code + 1, 0)
    return jnp.sum(place, axis=0, keepdims=True) - 1


def one_hot(index, size):
    shape = (16, index.shape[1])
    away = iota(shape, 0).astype(F32).astype(BF16)
    away = away - jnp.broadcast_to(index.astype(F32), shape).astype(BF16)
    one, zero = jnp.ones(shape, BF16), jnp.zeros(shape, BF16)
    return jnp.concatenate(
        [jnp.where(away == jnp.full(shape, -16.0 * b, BF16), one, zero) for b in range(size // 16)],
        axis=0,
    )


def pack_operand(payload):
    return jnp.concatenate(parts_wide(payload), axis=0).astype(BF16)


def slots_hot(slots):
    return jnp.concatenate([one_hot(slots, 256), one_hot(slots - 256, 128)], axis=0)


def scatter_operand(values, masses, cells):
    high, low = parts_wide(values * masses)
    stacked = jnp.concatenate([high, low], axis=0)
    upper = (cells >> 8).astype(F32)
    return jnp.concatenate([stacked * (1.0 - upper), stacked * upper], axis=0).astype(BF16)


def scatter(group):
    hot = [one_hot(cells & 255, 4 * PLANE) for _, _, cells in group]
    left = [scatter_operand(*one) for one in group]
    return sum(dot_nt(a, b) for a, b in zip(left, hot))


def by_cell(result):
    pieces = []
    for x in range(SIDE):
        base = 2 * ROWS * (x // 4)
        lanes = slice(PLANE * (x % 4), PLANE * (x % 4 + 1))
        pieces.append(result[base : base + ROWS, lanes] + result[base + ROWS : base + 2 * ROWS, lanes])
    return jnp.concatenate(pieces, axis=0)


def average(sums, field):
    pieces = []
    for x in range(SIDE):
        rows = slice(ROWS * x, ROWS * (x + 1))
        one, old = sums[rows], field[rows]
        new = (one + PRIOR_MASS * old) / (one[20:21] + PRIOR_MASS)
        pieces.append(jnp.where(iota(new.shape, 0) == 20, old, new))
    return jnp.concatenate(pieces, axis=0)


def kernel(sizes, *refs):
    inputs, out_ref, refs = refs[:INPUTS], refs[INPUTS], refs[INPUTS + 1 :]
    local, refs = refs[:INPUTS], refs[INPUTS:]
    (
        plane,
        z_send,
        c_send,
        x_send,
        tile_got,
        row_got,
        x_got,
        packed,
        got,
        rows_buf,
        pay,
        local_sem,
        halo_send_sem,
        halo_recv_sem,
        move_send_sem,
        move_recv_sem,
    ) = refs
    n_gx, n_gy, n_gz = sizes
    gx, gy, gz = lax.axis_index("gx"), lax.axis_index("gy"), lax.axis_index("gz")

    def three(index, size):
        return {-1: lax.rem(index + size - 1, size), 0: index, 1: lax.rem(index + 1, size)}

    near_x, near_y, near_z = three(gx, n_gx), three(gy, n_gy), three(gz, n_gz)

    def at(dx, dy, dz):
        return near_x[dx], near_y[dy], near_z[dz]

    faces = [(1, 0), (-1, 0), (0, 1), (0, -1)]
    corners = [(1, 1), (1, -1), (-1, 1), (-1, -1)]
    x_steps = [1, -1]
    halo_steps = [(dx, dy, dz) for dx in x_steps for dy, dz in corners]
    halo_steps += [(0, dy, dz) for dy, dz in corners]
    halo_steps += [(dx, dy, 0) for dx in x_steps for dy in (1, -1)]
    halo_steps += [(0, dy, 0) for dy in (1, -1)]
    halo_steps += [(dx, 0, dz) for dx in x_steps for dz in (1, -1)]
    halo_steps += [(0, 0, dz) for dz in (1, -1)]
    halo_steps += [(dx, 0, 0) for dx in x_steps]

    loads = {
        name: pltpu.make_async_copy(a, to, local_sem.at[i])
        for i, (name, a, to) in enumerate(zip(NAMES, inputs, local))
    }
    barrier = pltpu.get_barrier_semaphore()
    for step in halo_steps:
        pl.semaphore_signal(barrier, inc=1, device_id=at(*step), device_id_type=MESH)
    for name in ORDER:
        loads[name].start()

    def load(name):
        loads[name].wait()
        return local[NAMES.index(name)]

    def remote_copy(src, dst, send_sem, recv_sem, step):
        return pltpu.make_async_remote_copy(
            src_ref=src,
            dst_ref=dst,
            send_sem=send_sem,
            recv_sem=recv_sem,
            device_id=at(*step),
            device_id_type=MESH,
        )

    def put(h, value):
        plane[h, 0] = value[:, :128]
        plane[h, 1] = value[:, 128:]

    def all_of(buffer, send_sem, recv_sem):
        return remote_copy(buffer, buffer, send_sem, recv_sem, (1, 0, 0))

    def halo_kind(h, kind):
        buffer = (tile_got, row_got, x_got)[kind].at[h]
        return all_of(buffer, halo_send_sem.at[h, kind], halo_recv_sem.at[h, kind])

    def send_halo(h, first, kind, source, target):
        for i, (src, dst) in enumerate(zip(source, target)):
            remote_copy(
                src, dst, halo_send_sem.at[h, kind], halo_recv_sem.at[h, kind], halo_steps[first + i]
            ).start()

    def prepare_x(h, field):
        x_send[h, 0, :, 0:PLANE] = field[7 * ROWS : 8 * ROWS]
        x_send[h, 1, :, 0:PLANE] = field[0:ROWS]

    def send_x(h):
        send_halo(h, 24, 2, [x_send.at[h, k] for k in range(2)], [x_got.at[h, k] for k in range(2)])

    def prepare_corners(h):
        for slot, row in enumerate((63, 56, 7, 0)):
            for half in range(2):
                c_send[h, slot, half] = plane[h, half, row : row + 1, :]

    def prepare_z(h):
        for z, slot in ((7, 0), (0, 1)):
            for half in range(2):
                z_send[h, slot, half] = plane[h, half, pl.ds(z, SIDE, stride=SIDE), :]

    def send_y(h):
        sides = ((0, 1), (1, 0))
        source = [c_send.at[h, slot, half] for _, half in sides for slot in range(4)]
        target = [row_got.at[h, 8 + 4 * k + slot] for k, _ in sides for slot in range(4)]
        source += [c_send.at[h, slot] for slot in range(4)]
        target += [row_got.at[h, 2 * slot : 2 * slot + 2] for slot in range(4)]
        send_halo(h, 0, 1, source, target)
        rows = plane.at[h]
        y_rows = (slice(56, 64), slice(0, 8))
        source = [rows.at[half, y] for _, half in sides for y in y_rows]
        target = [tile_got.at[h, 8 + 4 * k + slot] for k, _ in sides for slot in range(2)]
        source += [rows.at[:, y] for y in y_rows]
        target += [tile_got.at[h, 2 * slot : 2 * slot + 2] for slot in range(2)]
        send_halo(h, 12, 0, source, target)

    def send_z(h):
        sides = ((0, 1), (1, 0))
        source = [z_send.at[h, slot, half] for _, half in sides for slot in range(2)]
        target = [tile_got.at[h, 10 + 4 * k + slot] for k, _ in sides for slot in range(2)]
        source += [z_send.at[h, slot] for slot in range(2)]
        target += [tile_got.at[h, 4 + 2 * slot : 6 + 2 * slot] for slot in range(2)]
        send_halo(h, 18, 0, source, target)

    def stack_outer(face, corner):
        row = iota((SIDE, 128), 0)
        last = jnp.zeros((SIDE, 128), F32)
        for slot in range(4):
            last = jnp.where(row == slot, corner[slot], last)
        none = jnp.zeros((PLANE - 5 * SIDE, 128), F32)
        return jnp.concatenate(face + [last, none], axis=0)

    def inner_left(h, field):
        halo_kind(h, 2).wait_recv()
        sides = jnp.concatenate([x_got[h, 0], x_got[h, 1]], axis=0)[:, :PLANE]
        return jnp.concatenate([left_of(field), left_of(sides)], axis=0)

    def outer_left(h):
        for kind in range(2):
            halo_kind(h, kind).wait_recv()
        both = [
            stack_outer(
                [tile_got[h, 2 * slot + half] for slot in range(4)],
                [row_got[h, 2 * slot + half] for slot in range(4)],
            )
            for half in range(2)
        ]
        side = [
            stack_outer(
                [tile_got[h, 8 + 4 * k + slot] for slot in range(4)],
                [row_got[h, 8 + 4 * k + slot] for slot in range(4)],
            )
            for k in range(2)
        ]
        last = jnp.where(iota((PLANE, 128), 1) < PLANE, side[1], side[0])
        return left_outer(jnp.concatenate(both + [last], axis=1))

    lower = iota((16, 128), 1) < BLOCK

    def turned(value):
        return pltpu.roll(value, BLOCK, 1)

    def move_sems(m, first):
        return move_send_sem.at[m, first // 4], move_recv_sem.at[m, first // 4]

    def moves(m, first):
        return all_of(got.at[m, 4:6] if first else got.at[m, 0:4], *move_sems(m, first))

    def send_moves(m, first, block):
        for t in range(block.shape[1] // 128):
            tile = block[:, 128 * t : 128 * (t + 1)]
            k = first + 2 * t
            packed[m, k] = jnp.where(lower, tile[:16], turned(tile[16:]))
            packed[m, k + 1] = jnp.where(lower, turned(tile[:16]), tile[16:])
            for i in (k, k + 1):
                remote_copy(
                    packed.at[m, i], got.at[m, i], *move_sems(m, first), MOVE_STEPS[i]
                ).start()

    def arrivals(m, first):
        moves(m, first).wait_recv()
        tiles = []
        for k in (4,) if first else (0, 2):
            one, two = got[m, k], got[m, k + 1]
            top = jnp.where(lower, one, turned(two))
            bottom = jnp.where(lower, turned(one), two)
            tiles.append(jnp.concatenate([top, bottom], axis=0))
        return jnp.concatenate(tiles, axis=1)

    def sent(h):
        for kind in range(3):
            halo_kind(h, kind).wait_send()

    plane[0] = jnp.zeros((2, PLANE, 128), F32)
    x_send[...] = jnp.zeros(x_send.shape, F32)
    same_z = jnp.where(iota((PLANE, SIDE), 0) & 7 == iota((PLANE, SIDE), 1), 1.0, 0.0)
    same_y = iota((PLANE, PLANE), 0) >> 3 == iota((PLANE, PLANE), 1) & 7
    goes = (iota((PLANE, SIDE * LANES), 0) >> 3) * LANES + 20
    goes = jnp.where(iota((PLANE, SIDE * LANES), 1) == goes, 1.0, 0.0).astype(BF16)
    rate = jnp.zeros((PLANE, SIDE * LANES), F32)
    for part in parts(load("mix_rate")[...]):
        along_z = jnp.where(same_y, dot_nt(same_z.astype(BF16), part), 0.0)
        rate = rate + dot(along_z.astype(BF16), goes)
    mean_ref = load("mean_field")
    for x in range(SIDE):
        base = LANES * (x % 4)
        plane[0, x // 4, :, base : base + 20] = mean_ref[PLANE * x : PLANE * (x + 1), :]
    inner1 = jnp.concatenate([plane[0, 0], plane[0, 1]], axis=1) + rate
    put(0, inner1)
    prepare_corners(0)
    prepare_z(0)
    field1 = compact(inner1.T)
    prepare_x(0, field1)

    pl.semaphore_wait(barrier, len(halo_steps))
    send_y(0)
    send_x(0)
    send_z(0)

    ok = [
        jnp.where(gx > 0, 1.0, 0.0),
        jnp.where(gx < n_gx - 1, 1.0, 0.0),
        jnp.where(gy > 0, 1.0, 0.0),
        jnp.where(gy < n_gy - 1, 1.0, 0.0),
    ]

    cell1 = load("cell_first")
    off1 = load("offset_first")
    face1 = load("face_first")
    cell2 = load("cell_second")
    cell3 = load("cell_final")
    mass = load("particle_mass")
    off2 = load("offset_second")
    pay[0:20, :] = load("scalars")[...]
    pay[20:21, :] = mass[...]
    pay[21:24, :] = off2[...]
    pay[24:25, :] = cell2[...].astype(F32)
    pay[25:26, :] = cell3[...].astype(F32)
    pay[26:27, :] = cell1[...].astype(F32)
    pay[27:30, :] = off1[...]
    pay[30:32, :] = jnp.zeros((2, pay.shape[1]), F32)

    def packed_movers(faces):
        slots = slots_of(faces)
        hot = [slots_hot(slots[:, lanes]) for lanes in OWN]
        left = [pack_operand(pay[:, lanes]) for lanes in OWN]
        block = sum(dot_nt(a, b) for a, b in zip(left, hot))
        return block[:32] + block[32:]

    def weights_at(cells, offsets, lanes):
        return weights(cells[:, lanes], [offsets[d : d + 1, lanes] for d in range(3)], ok)

    def scalars_of(block):
        row = iota((ROWS, block.shape[1]), 0)
        return jnp.where(row == 20, 1.0, jnp.where(row < 20, block[:ROWS], 0.0))

    def message(values, block):
        row = iota((ROWS, block.shape[1]), 0)
        return jnp.concatenate([jnp.where(row < 20, values, block[:ROWS]), block[ROWS:]], axis=0)

    def work(values, sampled, outer, ws):
        more = gather(outer, ws, 1)
        return react(values, [a + b for a, b in zip(sampled, more)], first, second)

    def work_movers(m, movers, inner, outer, ws):
        for i, (first, lanes) in enumerate(((4, FAR), (0, NEAR))):
            block = movers[:, lanes]
            new = work([scalars_of(block)], inner[i : i + 1], outer, ws[i : i + 1])
            send_moves(m, first, message(new[0], block))

    movers = packed_movers(face1[...])
    mover_cells = movers[26:27].astype(jnp.int32)
    w_movers = [weights_at(mover_cells, movers[27:30], lanes) for lanes in (FAR, NEAR)]

    rows_buf[...] = jnp.zeros(rows_buf.shape, F32)
    rows_buf[0, 0:20, :] = load("react_in")[...]
    rows_buf[0, 20:21, :] = load("hidden_bias")[...]
    rows_buf[1, 0:20, :] = load("react_out")[...]
    high, low = parts_wide(rows_buf[0])
    first = jnp.concatenate(
        [high, high, low, jnp.zeros((128 - 3 * ROWS, 128), F32)], axis=0
    ).T.astype(BF16)
    high, low = parts_wide(rows_buf[1])
    second = jnp.concatenate(
        [
            jnp.concatenate([high, high], axis=1),
            jnp.concatenate([low, jnp.zeros_like(low)], axis=1),
        ],
        axis=0,
    ).astype(BF16)

    w_own = [weights_at(cell1, off1, lanes) for lanes in OWN]
    left = inner_left(0, field1)
    in_movers = gather(left, w_movers, 0)
    in_own = gather(left, w_own, 0)

    outer = outer_left(0)
    work_movers(0, movers, in_movers, outer, w_movers)

    values = work([scalars_of(pay[:, lanes]) for lanes in OWN], in_own, outer, w_own)
    stay = [jnp.where(face1[:, lanes] == 0, mass[:, lanes], 0.0) for lanes in OWN]
    sums = scatter([(v, m, cell2[:, lanes]) for v, m, lanes in zip(values, stay, OWN)])
    for one, lanes in zip(values, OWN):
        pay[0:20, lanes] = one[:20]

    lane = iota((1, 128), 1)
    alive = {
        0: jnp.concatenate([jnp.where(lane < 64, ok[0], ok[1]), jnp.ones((1, 128), F32)], axis=1),
        4: jnp.where(lane < 64, ok[2], ok[3]),
    }

    came = {}
    for i in (0, 4):
        block = arrivals(0, i)
        came[i] = block
        cells = block[24:25].astype(jnp.int32)
        sums = sums + scatter([(scalars_of(block), block[20:21] * alive[i], cells)])
    field2 = average(by_cell(sums), field1)
    put(1, spread(field2).T)
    prepare_corners(1)
    send_y(1)
    prepare_x(1, field2)
    send_x(1)
    prepare_z(1)
    send_z(1)

    face2 = load("face_second")
    movers = packed_movers(face2[...])
    mover_cells = movers[24:25].astype(jnp.int32)
    w_movers = [weights_at(mover_cells, movers[21:24], lanes) for lanes in (FAR, NEAR)]
    w_own = [weights_at(cell2, off2, lanes) for lanes in OWN]
    w_own += [
        weights_at(block[24:25].astype(jnp.int32), block[21:24], slice(None))
        for block in came.values()
    ]
    left = inner_left(1, field2)
    in_movers = gather(left, w_movers, 0)
    in_own = gather(left, w_own, 0)

    outer = outer_left(1)
    work_movers(1, movers, in_movers, outer, w_movers)

    values = work(values + [scalars_of(block) for block in came.values()], in_own, outer, w_own)
    masses = [
        jnp.where(face1[:, lanes] + face2[:, lanes] == 0, mass[:, lanes], 0.0) for lanes in OWN
    ] + [block[20:21] * alive[i] for i, block in came.items()]
    cells = [cell3[:, lanes] for lanes in OWN]
    cells += [block[25:26].astype(jnp.int32) for block in came.values()]
    sums = scatter(list(zip(values, masses, cells)))

    sent(0)
    sent(1)
    for i in (0, 4):
        moves(0, i).wait_send()

    for i in (0, 4):
        block = arrivals(1, i)
        cells = block[25:26].astype(jnp.int32)
        sums = sums + scatter([(scalars_of(block), block[20:21] * alive[i], cells)])
    sums = by_cell(sums)
    result = spread(average(sums, field2)).T
    for x in range(SIDE):
        out_ref[PLANE * x : PLANE * (x + 1), :] = result[:, LANES * x : LANES * x + 20]

    for i in (0, 4):
        moves(1, i).wait_send()


def shards(
    sizes,
    scalars,
    particle_mass,
    cell_first,
    cell_second,
    cell_final,
    offset_first,
    offset_second,
    face_first,
    face_second,
    mean_field,
    mix_rate,
    react_in,
    hidden_bias,
    react_out,
):
    row = lambda a: a.reshape(1, -1)
    operands = [
        scalars,
        row(particle_mass),
        row(cell_first),
        row(cell_second),
        row(cell_final),
        offset_first,
        offset_second,
        row(face_first),
        row(face_second),
        mean_field.transpose(1, 2, 3, 0).reshape(SIDE * PLANE, 20),
        mix_rate.reshape(PLANE, SIDE),
        react_in.T,
        row(hidden_bias),
        react_out,
    ]
    operands = [pltpu.with_memory_space_constraint(a, pltpu.HBM) for a in operands]
    vmem = pl.BlockSpec(memory_space=pltpu.VMEM)
    result = pl.pallas_call(
        functools.partial(kernel, sizes),
        out_shape=jax.ShapeDtypeStruct((SIDE * PLANE, 20), F32),
        in_specs=[pl.BlockSpec(memory_space=pltpu.HBM)] * len(operands),
        out_specs=vmem,
        scratch_shapes=[pltpu.VMEM(a.shape, a.dtype) for a in operands]
        + [
            pltpu.VMEM((2, 2, PLANE, 128), F32),
            pltpu.VMEM((2, 2, 2, SIDE, 128), F32),
            pltpu.VMEM((2, 4, 2, 1, 128), F32),
            pltpu.VMEM((2, 2, ROWS, 128), F32),
            pltpu.VMEM((2, 16, SIDE, 128), F32),
            pltpu.VMEM((2, 16, 1, 128), F32),
            pltpu.VMEM((2, 2, ROWS, 128), F32),
            pltpu.VMEM((2, 6, 16, 128), F32),
            pltpu.VMEM((2, 6, 16, 128), F32),
            pltpu.VMEM((2, ROWS, 128), F32),
            pltpu.VMEM((32, 1024), F32),
            pltpu.SemaphoreType.DMA((INPUTS,)),
            pltpu.SemaphoreType.DMA((2, 3)),
            pltpu.SemaphoreType.DMA((2, 3)),
            pltpu.SemaphoreType.DMA((2, 2)),
            pltpu.SemaphoreType.DMA((2, 2)),
        ],
        compiler_params=pltpu.CompilerParams(
            collective_id=0, has_side_effects=True, vmem_limit_bytes=40 * 1024 * 1024
        ),
    )(*operands)
    return result.reshape(SIDE, SIDE, SIDE, 20).transpose(3, 0, 1, 2)


def solution(mesh):
    particles = P(("gx", "gy", "gz"))
    in_specs = (
        P(None, ("gx", "gy", "gz")),
        particles,
        particles,
        particles,
        particles,
        P(None, ("gx", "gy", "gz")),
        P(None, ("gx", "gy", "gz")),
        particles,
        particles,
        P(None, "gx", "gy", "gz"),
        P("gx", "gy", "gz"),
        P(),
        P(),
        P(),
    )
    sizes = (mesh.shape["gx"], mesh.shape["gy"], mesh.shape["gz"])
    return jax.shard_map(
        functools.partial(shards, sizes),
        mesh=mesh,
        in_specs=in_specs,
        out_specs=P(None, "gx", "gy", "gz"),
        check_vma=False,
    )
```
